32 devices in a mesh: tgt: 4 (over y, x), inner: 8 (over z, core).
Axes of the slice: x: 2, y: 2, z: 4, core: 2. Of those that a mesh axis runs over, the one named last changes fastest.
Arguments:
- near_tiles: bfloat16 [128, 1024, 1024], P(('tgt', 'inner')), may hold values from -0.1875 to 0.1875
- near_target: int32 [128], P(('tgt', 'inner')), may hold values from 0 to 7
- near_right: int32 [128], P(('tgt', 'inner')), may hold values from 0 to 31
- near_count: int32 [32], P(('tgt', 'inner')), may hold values from 1 to 4, as said below
- low_u: bfloat16 [1024, 64, 1024], P(('tgt', 'inner')), may hold values from -0.75 to 0.75
- low_v: bfloat16 [1024, 64, 1024], P(('tgt', 'inner')), may hold values from -0.1875 to 0.1875
- low_target: int32 [1024], P(('tgt', 'inner')), may hold values from 0 to 7, as said below
- low_right: int32 [1024], P(('tgt', 'inner')), may hold values from 0 to 31
- right_u: bfloat16 [256, 64, 1024], P(('tgt', 'inner')), may hold values from -6 to 6
- right_v: bfloat16 [256, 64, 1024], P(('tgt', 'inner')), may hold values from -0.25 to 0.25
- probe_seed: int32 [32], P('tgt'), may hold values from 1 to 29999
Outputs:
- basis_out: float32 [32, 64, 1024], P('tgt', None, 'inner')
- image_out: float32 [32, 64, 1024], P('tgt', None, 'inner')
The draws below stay inside these ranges and needn't reach their ends.
Inputs may be any that keep to these rules, and one draw needn't show every extreme that they name: `near_count`: some device holds 4 live slots. `low_target`: the 32 low-rank pairs of each device name every target tile of its group.
All inputs are finite; a program needn't handle non-finite values.
Results may differ from the reference program's by a relative error of at most 0.004.
Values may be sent and summed in bfloat16 or wider, within the bound.
A program may use at most 128 MiB of HBM per device.

```python
import math
import jax
import jax.numpy as jnp
from jax import lax

B = 1024
R = 64
TILE_GRP = 8
NEAR_MAX = 4
LOW_DEV = 32
RIGHT_DEV = 8
TGT_TILES = 32
RIGHT_SEG = 32
NEAR_ALL = 128
LOW_ALL = 1024
RIGHT_ALL = 256
N_TGT = 4
N_INNER = 8


def draw_near_count(key, part):
    dev_count = NEAR_ALL // NEAR_MAX
    first_key, second_key = jax.random.split(jax.random.fold_in(key, 11))
    counts = jax.random.randint(first_key, (dev_count,), 1, NEAR_MAX + 1)
    busiest = jax.random.randint(second_key, (), 0, dev_count)
    return jnp.where(jnp.arange(dev_count) == busiest, NEAR_MAX, counts).astype(jnp.int32)


def draw_low_target(key, part):
    dev_count = LOW_ALL // LOW_DEV
    offsets = jax.random.randint(jax.random.fold_in(key, 23), (dev_count, 1), 0, TILE_GRP)
    slot_index = jnp.arange(LOW_DEV)[None, :]
    return ((slot_index + offsets) % TILE_GRP).reshape(-1).astype(jnp.int32)


def place_ends(values, key, least, largest):
    longest = values.shape.index(max(values.shape))
    spots = []
    for shift in (0, 1):
        where = [jax.random.randint(jax.random.fold_in(key, axis), (), 0, length) for axis, length in enumerate(values.shape)]
        where[longest] = (where[longest] + shift) % values.shape[longest]
        spots.append(tuple(where))
    return values.at[spots[0]].set(least).at[spots[1]].set(largest)


def steps_of(stream_key, shape, shards, low, largest):
    def one(position, parts):
        draws = jax.random.uniform(jax.random.fold_in(jax.random.fold_in(stream_key, 6), position), (parts,), jnp.float32, low / len(shards), largest / len(shards))
        return jnp.repeat(jnp.exp(draws), shape[position] // parts).reshape((-1,) + (1,) * (len(shape) - position - 1))

    level = one(*shards[0])
    for cut in shards[1:]:
        level = level * one(*cut)
    return level


def bell_draw(own_key, dims, scale, limit, cuts=(), kind=jnp.bfloat16):
    entries = jax.random.normal(own_key, dims, jnp.float32) * scale
    if len(cuts) > 0:
        entries = steps_of(own_key, dims, cuts, -0.22, 0.18) * entries
    return jnp.clip(entries, min=-limit, max=limit).astype(kind)


def setup_inputs(seed: int = 0) -> dict:
    splits = jax.random.split(jax.random.key(seed), 12)
    near_tiles = bell_draw(splits[0], (NEAR_ALL, B, B), B ** -0.5, 0.1875, ((0, 32),))
    near_target = place_ends(jax.random.randint(splits[1], (NEAR_ALL,), 0, TILE_GRP), jax.random.fold_in(splits[1], 1), 0, TILE_GRP - 1).astype(jnp.int32)
    near_right = place_ends(jax.random.randint(splits[2], (NEAR_ALL,), 0, RIGHT_SEG), jax.random.fold_in(splits[2], 1), 0, RIGHT_SEG - 1).astype(jnp.int32)
    near_count = draw_near_count(jax.random.fold_in(splits[11], 71), 0)
    low_u = bell_draw(splits[4], (LOW_ALL, R, B), R ** -0.5, 0.75, ((0, 32),))
    low_v = bell_draw(splits[5], (LOW_ALL, R, B), B ** -0.5, 0.1875, ((0, 32),))
    low_target = draw_low_target(jax.random.fold_in(splits[11], 71), 0)
    low_right = place_ends(jax.random.randint(splits[7], (LOW_ALL,), 0, RIGHT_SEG), jax.random.fold_in(splits[7], 1), 0, RIGHT_SEG - 1).astype(jnp.int32)
    right_u = bell_draw(splits[8], (RIGHT_ALL, R, B), 1.0, 6.0, ((0, 32),))
    right_v = bell_draw(splits[9], (RIGHT_ALL, R, B), (R * N_INNER) ** -0.5, 0.25, ((0, 32),))
    probe_seed = place_ends(jax.random.randint(splits[10], (TGT_TILES,), 1, 30000), jax.random.fold_in(splits[10], 1), 1, 29999).astype(jnp.int32)
    return {"near_tiles": near_tiles, "near_target": near_target, "near_right": near_right, "near_count": near_count, "low_u": low_u, "low_v": low_v, "low_target": low_target, "low_right": low_right, "right_u": right_u, "right_v": right_v, "probe_seed": probe_seed}


HIGHEST = lax.Precision.HIGHEST

def probe_table(seeds, rank_size, order):
    shape = (seeds.shape[0], rank_size, order)
    chan = lax.broadcasted_iota(jnp.int32, shape, 1)
    place = lax.broadcasted_iota(jnp.int32, shape, 2)
    code = (seeds[:, None, None] * 9973 + place * place * 7 + place * chan * 131 + chan * chan * 17 + place * 7919 + chan * 104729) % 65521
    return ((code.astype(jnp.float32) - 32760.0) / 32768.0).astype(jnp.bfloat16)

def solve_one(chol_factor, sketch_tile):
    return jax.scipy.linalg.solve_triangular(chol_factor, sketch_tile, lower=True)

def orthonormal(sketch):
    gram = jnp.einsum('tdi,tei->tde', sketch, sketch, precision=HIGHEST)
    factor = jnp.linalg.cholesky(gram)
    return jax.vmap(solve_one)(factor, sketch)

def reference(near_tiles, near_target, near_right, near_count, low_u, low_v, low_target, low_right, right_u, right_v, probe_seed):
    dev_count = N_TGT * N_INNER
    near_blocks = near_tiles.reshape(dev_count, NEAR_MAX, B, B)
    near_tgt = near_target.reshape(dev_count, NEAR_MAX)
    near_rgt = near_right.reshape(dev_count, NEAR_MAX)
    low_u_all = low_u.reshape(dev_count, LOW_DEV, R, B)
    low_v_all = low_v.reshape(dev_count, LOW_DEV, R, B)
    low_tgt = low_target.reshape(dev_count, LOW_DEV)
    low_rgt = low_right.reshape(dev_count, LOW_DEV)
    right_u_all = right_u.reshape(N_TGT, N_INNER, RIGHT_DEV, R, B)
    right_v_all = right_v.reshape(N_TGT, N_INNER, RIGHT_DEV, R, B)
    probe_all = probe_table(probe_seed, R, B)

    def terms(device):
        group = device // N_INNER
        segment = device % N_INNER
        seg_u = jnp.take(right_u_all, segment, axis=1).reshape(N_TGT * RIGHT_DEV, R, B)
        seg_v = jnp.take(right_v_all, segment, axis=1).reshape(N_TGT * RIGHT_DEV, R, B)
        near_ub = seg_u[near_rgt[device]]
        near_vb = seg_v[near_rgt[device]]
        low_ub = seg_u[low_rgt[device]]
        low_vb = seg_v[low_rgt[device]]
        live_mask = (jnp.arange(NEAR_MAX, dtype=jnp.int32) < near_count[device]).astype(jnp.float32)
        near_left = jnp.einsum('jck,jik->jci', near_ub.astype(jnp.float32), near_blocks[device].astype(jnp.float32), precision=HIGHEST) * live_mask[:, None, None]
        mixing = jnp.einsum('jak,jck->jac', low_v_all[device].astype(jnp.float32), low_ub.astype(jnp.float32), precision=HIGHEST).astype(jnp.bfloat16)
        low_left = jnp.einsum('jac,jai->jci', mixing.astype(jnp.float32), low_u_all[device].astype(jnp.float32), precision=HIGHEST)
        left_fac = jnp.concatenate([near_left, low_left], axis=0)
        right_fac = jnp.concatenate([near_vb, low_vb], axis=0).astype(jnp.float32)
        targets = jnp.concatenate([near_tgt[device], low_tgt[device]], axis=0).astype(jnp.int32)
        onehot = (targets[:, None] == jnp.arange(TILE_GRP, dtype=jnp.int32)[None, :]).astype(jnp.float32)
        return (group, left_fac, right_fac, targets, onehot)

    def sketch_step(carried, device):
        group, left_fac, right_fac, targets, onehot = terms(device)
        probe = lax.dynamic_slice_in_dim(probe_all, group * TILE_GRP, TILE_GRP, 0)
        zeta = jnp.einsum('jck,jdk->jcd', right_fac, probe[targets].astype(jnp.float32), precision=HIGHEST)
        ypair = jnp.einsum('jcd,jci->jdi', zeta, left_fac, precision=HIGHEST)
        sketch = jnp.einsum('jt,jdi->tdi', onehot, ypair, precision=HIGHEST)
        before = lax.dynamic_slice_in_dim(carried, group * TILE_GRP, TILE_GRP, 0)
        return (lax.dynamic_update_slice_in_dim(carried, before + sketch, group * TILE_GRP, 0), None)
    devices = jnp.arange(dev_count, dtype=jnp.int32)
    zeros = jnp.zeros((TGT_TILES, R, B), jnp.float32)
    sketch_total, unused = lax.scan(sketch_step, zeros, devices)
    basis = orthonormal(sketch_total)

    def image_step(carried, device):
        group, left_fac, right_fac, targets, onehot = terms(device)
        basis_grp = lax.dynamic_slice_in_dim(basis, group * TILE_GRP, TILE_GRP, 0)
        proj = jnp.einsum('jci,jdi->jcd', left_fac, basis_grp[targets], precision=HIGHEST)
        image = jnp.einsum('jcd,jck->jdk', proj, right_fac, precision=HIGHEST)
        tile_image = jnp.einsum('jt,jdk->tdk', onehot, image, precision=HIGHEST)
        before = lax.dynamic_slice_in_dim(carried, group * TILE_GRP, TILE_GRP, 0)
        return (lax.dynamic_update_slice_in_dim(carried, before + tile_image, group * TILE_GRP, 0), None)
    image_total, unused_two = lax.scan(image_step, zeros, devices)
    return (basis * math.sqrt(B), image_total)
```

```python
import functools
import math

import jax
import jax.numpy as jnp
from jax import lax
from jax.experimental import pallas as pl
from jax.experimental.pallas import tpu as pltpu
from jax.sharding import PartitionSpec as P

HIGHEST = lax.Precision.HIGHEST
MESH = pl.DeviceIdType.MESH
F32 = jnp.float32
BF16 = jnp.bfloat16
VMEM_LIMIT = 56 * 1024 * 1024


def nt_dot(a, b):
    return lax.dot_general(a, b, (((1,), (1,)), ((), ())), preferred_element_type=F32)


def nn_dot(a, b):
    return lax.dot_general(a, b, (((1,), (0,)), ((), ())), preferred_element_type=F32)


def split(x):
    hi = x.astype(BF16)
    return hi, (x - hi.astype(F32)).astype(BF16)


def probe_table(seeds, rank_size, order):
    shape = (seeds.shape[0], rank_size, order)
    chan = lax.broadcasted_iota(jnp.int32, shape, 1)
    place = lax.broadcasted_iota(jnp.int32, shape, 2)
    code = (
        seeds[:, None, None] * 9973
        + place * place * 7
        + place * chan * 131
        + chan * chan * 17
        + place * 7919
        + chan * 104729
    ) % 65521
    return ((code.astype(F32) - 32760.0) / 32768.0).astype(BF16)


def gather_kernel(nt, u_ref, v_ref, su_ref, sv_ref, send, recv, local):
    me = lax.axis_index("tgt")
    k = u_ref.shape[0]
    mine = pl.ds(me * k, k)
    lu = pltpu.make_async_copy(u_ref, su_ref.at[mine], local.at[0])
    lv = pltpu.make_async_copy(v_ref, sv_ref.at[mine], local.at[1])
    lu.start()
    lv.start()
    barrier = pltpu.get_barrier_semaphore()

    def push(src, dst, sem, to):
        copy = pltpu.make_async_remote_copy(
            src_ref=src,
            dst_ref=dst,
            send_sem=send.at[sem],
            recv_sem=recv.at[sem],
            device_id={"tgt": to},
            device_id_type=MESH,
        )
        copy.start()
        return copy

    copies = []
    if nt == 4:
        a = me + 1 - 2 * (me % 2)
        b = (me + 2) % 4
        for peer in (a, b):
            pl.semaphore_signal(barrier, inc=1, device_id={"tgt": peer}, device_id_type=MESH)
        pl.semaphore_wait(barrier, 2)
        ua = push(u_ref, su_ref.at[mine], 0, a)
        vb = push(v_ref, sv_ref.at[mine], 1, b)
        va = push(v_ref, sv_ref.at[mine], 2, a)
        ub = push(u_ref, su_ref.at[mine], 3, b)
        from_a = pl.ds(a * k, k)
        from_b = pl.ds(b * k, k)
        ua.wait_recv()
        fu = push(su_ref.at[from_a], su_ref.at[from_a], 4, b)
        vb.wait_recv()
        fv = push(sv_ref.at[from_b], sv_ref.at[from_b], 5, a)
        for c in (va, ub, fu, fv):
            c.wait_recv()
        copies = [ua, vb, va, ub, fu, fv]
    else:
        for d in range(1, nt):
            pl.semaphore_signal(
                barrier, inc=1, device_id={"tgt": (me + d) % nt}, device_id_type=MESH
            )
        pl.semaphore_wait(barrier, nt - 1)
        for d in range(1, nt):
            to = (me + d) % nt
            copies.append(push(u_ref, su_ref.at[mine], 2 * d - 2, to))
            copies.append(push(v_ref, sv_ref.at[mine], 2 * d - 1, to))
        for c in copies:
            c.wait_recv()
    for c in copies:
        c.wait_send()
    lu.wait()
    lv.wait()


def gather_tiles(nt, u, v):
    sems = 6 if nt == 4 else max(2 * nt - 2, 1)
    shape = jax.ShapeDtypeStruct((nt * u.shape[0],) + u.shape[1:], u.dtype)
    return pl.pallas_call(
        functools.partial(gather_kernel, nt),
        out_shape=(shape, shape),
        in_specs=[pl.BlockSpec(memory_space=pl.ANY)] * 2,
        out_specs=[pl.BlockSpec(memory_space=pl.ANY)] * 2,
        scratch_shapes=[
            pltpu.SemaphoreType.DMA((sems,)),
            pltpu.SemaphoreType.DMA((sems,)),
            pltpu.SemaphoreType.DMA((2,)),
        ],
        compiler_params=pltpu.CompilerParams(collective_id=0, has_side_effects=True),
    )(u, v)


def reduce_kernel(n, gather, x_ref, *refs):
    if gather:
        out_ref, half, part, total, send, recv = refs
    else:
        out_ref, half, part, got_unused, send, recv = refs
    me = lax.axis_index("inner")
    m = n // 2
    z = me // 2
    core = me % 2
    other = 1 - core
    sib = z * 2 + other
    barrier = pltpu.get_barrier_semaphore()
    pl.semaphore_signal(barrier, inc=1, device_id={"inner": sib}, device_id_type=MESH)
    for d in range(1, m):
        peer = ((z + d) % m) * 2 + core
        pl.semaphore_signal(barrier, inc=1, device_id={"inner": peer}, device_id_type=MESH)
    pl.semaphore_wait(barrier, m)

    def push(src, dst, sem, to):
        copy = pltpu.make_async_remote_copy(
            src_ref=src,
            dst_ref=dst,
            send_sem=send.at[sem],
            recv_sem=recv.at[sem],
            device_id={"inner": to},
            device_id_type=MESH,
        )
        copy.start()
        return copy

    pairs = []
    for d in range(m):
        q = (z + 1 + d) % m
        pairs.append(push(x_ref.at[q, other], half.at[q], d, sib))
    sends = []
    for d in range(m):
        q = (z + 1 + d) % m
        pairs[d].wait_recv()
        half[q] = half[q] + x_ref[q, core]
        if d < m - 1:
            sends.append(push(half.at[q], part.at[m - 2 - d], m + d, q * 2 + core))
    acc = half[z]
    for d in range(m - 1):
        sends[d].wait_recv()
        acc = acc + part[m - 2 - d]
    if gather:
        total[...] = acc
        out_ref[z, core] = acc
        outs = [push(total, out_ref.at[z, core], 2 * m - 1, sib)]
        away = []
        for d in range(m - 1):
            q = (z + 1 + d) % m
            away.append(push(total, out_ref.at[z, core], 2 * m + d, q * 2 + core))
        for d in range(m - 1):
            q = (z + 2 * m - 1 - d) % m
            away[d].wait_recv()
            outs.append(push(out_ref.at[q, core], out_ref.at[q, core], 3 * m - 1 + d, sib))
        for c in outs:
            c.wait_recv()
        sends = sends + outs + away
    else:
        out_ref[...] = acc
    for c in pairs + sends:
        c.wait_send()


def reduce_inner(n, x, gather):
    m = n // 2
    block = x.shape[2:]
    sems = 4 * m - 2 if gather else 2 * m - 1
    return pl.pallas_call(
        functools.partial(reduce_kernel, n, gather),
        out_shape=jax.ShapeDtypeStruct(x.shape if gather else block, F32),
        in_specs=[pl.BlockSpec(memory_space=pltpu.VMEM)],
        out_specs=pl.BlockSpec(memory_space=pltpu.VMEM),
        scratch_shapes=[
            pltpu.VMEM((m,) + block, F32),
            pltpu.VMEM((max(m - 1, 1),) + block, F32),
            pltpu.VMEM(block, F32),
            pltpu.SemaphoreType.DMA((sems,)),
            pltpu.SemaphoreType.DMA((sems,)),
        ],
        compiler_params=pltpu.CompilerParams(
            collective_id=1 if gather else 2, has_side_effects=True, vmem_limit_bytes=VMEM_LIMIT
        ),
    )(x)


def near_sketch_kernel(right, target, count, near_ref, u_ref, v_ref, probe_ref, lh_ref, ll_ref, sk_ref):
    j = pl.program_id(0)

    @pl.when(j == 0)
    def _():
        sk_ref[...] = jnp.zeros_like(sk_ref)

    t = target[j]
    live = (j < count[0]).astype(F32)
    left = nt_dot(u_ref[0], near_ref[0]) * live
    lh, ll = split(left)
    lh_ref[0] = lh
    ll_ref[0] = ll
    zh, zl = split(nt_dot(probe_ref[t], v_ref[0]))
    sk_ref[t] += nn_dot(zh, lh) + nn_dot(zl, lh) + nn_dot(zh, ll)


def low_sketch_kernel(batch, right, target, *refs):
    u_refs, v_refs = refs[:batch], refs[batch : 2 * batch]
    low_u_ref, low_v_ref, probe_ref, base_ref, mix_ref, sk_ref = refs[2 * batch :]
    j = pl.program_id(0)

    @pl.when(j == 0)
    def _():
        sk_ref[...] = base_ref[...]

    terms = []
    for o in range(batch):
        t = target[j * batch + o]
        mixing = nt_dot(low_v_ref[o], u_refs[o][0]).astype(BF16)
        mix_ref[o] = mixing
        zh, zl = split(nt_dot(probe_ref[t], v_refs[o][0]))
        qh, ql = split(nt_dot(zh, mixing) + nt_dot(zl, mixing))
        low_u = low_u_ref[o]
        terms.append((t, nn_dot(qh, low_u) + nn_dot(ql, low_u)))
    for t, y in terms:
        sk_ref[t] += y


def add_columns(im_ref, t, y):
    n, share = im_ref.shape[0], im_ref.shape[3]
    for p in range(n):
        im_ref[p, t] += y[:, p * share : (p + 1) * share]


def near_image_kernel(right, target, lh_ref, ll_ref, v_ref, sh_ref, sl_ref, im_ref):
    j = pl.program_id(0)

    @pl.when(j == 0)
    def _():
        im_ref[...] = jnp.zeros_like(im_ref)

    t = target[j]
    sh = sh_ref[t]
    lh = lh_ref[0]
    ph, pll = split(nt_dot(sh, lh) + nt_dot(sl_ref[t], lh) + nt_dot(sh, ll_ref[0]))
    v = v_ref[0]
    add_columns(im_ref, t, nn_dot(ph, v) + nn_dot(pll, v))


def low_image_kernel(batch, right, target, *refs):
    v_refs = refs[:batch]
    low_u_ref, mix_ref, sh_ref, sl_ref, base_ref, im_ref = refs[batch:]
    j = pl.program_id(0)

    @pl.when(j == 0)
    def _():
        im_ref[...] = base_ref[...]

    terms = []
    for o in range(batch):
        t = target[j * batch + o]
        low_u = low_u_ref[o]
        wh, wl = split(nt_dot(sh_ref[t], low_u) + nt_dot(sl_ref[t], low_u))
        mixing = mix_ref[o]
        ph, pll = split(nn_dot(wh, mixing) + nn_dot(wl, mixing))
        v = v_refs[o][0]
        terms.append((t, nn_dot(ph, v) + nn_dot(pll, v)))
    for t, y in terms:
        add_columns(im_ref, t, y)


def chol_inv_kernel(s_ref, out_ref, a_ref):
    tiles, r, _ = s_ref.shape
    row = lax.broadcasted_iota(jnp.int32, (r, r), 0)
    col = lax.broadcasted_iota(jnp.int32, (r, r), 1)
    eye = (row == col).astype(F32)
    for t in range(tiles):
        s = s_ref[t]
        a_ref[t, :, :r] = lax.dot_general(
            s, s, (((1,), (1,)), ((), ())), precision=HIGHEST, preferred_element_type=F32
        )
        a_ref[t, :, r:] = eye
    rows = [a_ref[:, 8 * b : 8 * b + 8, :] for b in range(r // 8)]
    sub = lax.broadcasted_iota(jnp.int32, (tiles, 8, 2 * r), 1)
    for k in range(r):
        b0, e = k // 8, k % 8
        pivot = rows[b0][:, e : e + 1, :]
        inv = 1.0 / pivot[:, :, k : k + 1]
        scaled = pivot * inv
        for b in range(b0, r // 8):
            step = rows[b][:, :, k : k + 1] * scaled
            if b == b0:
                step = jnp.where(sub > e, step, 0.0)
            rows[b] = rows[b] - step
    lane = lax.broadcasted_iota(jnp.int32, (tiles, 8, 2 * r), 2)
    for b in range(r // 8):
        diag = jnp.sum(jnp.where(lane == sub + 8 * b, rows[b], 0.0), axis=2, keepdims=True)
        out_ref[:, 8 * b : 8 * b + 8, :] = (rows[b] * lax.rsqrt(diag))[:, :, r:]


def whole(shape):
    zeros = (0,) * len(shape)
    return pl.BlockSpec(shape, lambda j, *s: zeros)


def at_right(shape, batch, o):
    return pl.BlockSpec((1,) + shape[1:], lambda j, right, *s: (right[j * batch + o], 0, 0))


def per_step(batch, shape):
    return pl.BlockSpec((batch,) + shape[1:], lambda j, *s: (j,) + (0,) * (len(shape) - 1))


def run(kernel, scalars, steps, ins, specs, outs, out_specs):
    return pl.pallas_call(
        kernel,
        grid_spec=pltpu.PrefetchScalarGridSpec(
            num_scalar_prefetch=len(scalars), grid=(steps,), in_specs=specs, out_specs=out_specs
        ),
        out_shape=outs,
        compiler_params=pltpu.CompilerParams(vmem_limit_bytes=VMEM_LIMIT),
    )(*scalars, *ins)


def per_device(
    nt,
    ni,
    near_tiles,
    near_target,
    near_right,
    near_count,
    low_u,
    low_v,
    low_target,
    low_right,
    right_u,
    right_v,
    probe_seed,
):
    slots, order = near_tiles.shape[0], near_tiles.shape[1]
    lows, r = low_u.shape[0], low_u.shape[1]
    tiles = probe_seed.shape[0]
    share = order // ni
    batch = math.gcd(lows, 4)
    seg_u, seg_v = gather_tiles(nt, right_u, right_v)
    probe = probe_table(probe_seed, r, order)
    sk = jax.ShapeDtypeStruct((tiles, r, order), F32)
    left = jax.ShapeDtypeStruct((slots, r, order), BF16)
    lh, ll, near_sk = run(
        near_sketch_kernel,
        (near_right, near_target, near_count),
        slots,
        (near_tiles, seg_u, seg_v, probe),
        [
            per_step(1, near_tiles.shape),
            at_right(seg_u.shape, 1, 0),
            at_right(seg_v.shape, 1, 0),
            whole(probe.shape),
        ],
        (left, left, sk),
        (per_step(1, left.shape), per_step(1, left.shape), whole(sk.shape)),
    )
    mix_shape = jax.ShapeDtypeStruct((lows, r, r), BF16)
    mixing, sketch = run(
        functools.partial(low_sketch_kernel, batch),
        (low_right, low_target),
        lows // batch,
        (seg_u,) * batch + (seg_v,) * batch + (low_u, low_v, probe, near_sk),
        [at_right(seg_u.shape, batch, o) for o in range(batch)] * 2
        + [per_step(batch, low_u.shape), per_step(batch, low_v.shape)]
        + [whole(probe.shape), whole(sk.shape)],
        (mix_shape, sk),
        (per_step(batch, mix_shape.shape), whole(sk.shape)),
    )
    rows = tiles * r // ni
    total = reduce_inner(ni, sketch.reshape(ni // 2, 2, rows, order), True)
    total = total.reshape(tiles, r, order)
    sh, sl = split(total)
    im = jax.ShapeDtypeStruct((ni, tiles, r, share), F32)
    near_im = run(
        near_image_kernel,
        (near_right, near_target),
        slots,
        (lh, ll, seg_v, sh, sl),
        [
            per_step(1, lh.shape),
            per_step(1, ll.shape),
            at_right(seg_v.shape, 1, 0),
            whole(sh.shape),
            whole(sl.shape),
        ],
        im,
        whole(im.shape),
    )
    image = run(
        functools.partial(low_image_kernel, batch),
        (low_right, low_target),
        lows // batch,
        (seg_v,) * batch + (low_u, mixing, sh, sl, near_im),
        [at_right(seg_v.shape, batch, o) for o in range(batch)]
        + [per_step(batch, low_u.shape), per_step(batch, mixing.shape)]
        + [whole(sh.shape), whole(sl.shape), whole(im.shape)],
        im,
        whole(im.shape),
    )
    inverse = pl.pallas_call(
        chol_inv_kernel,
        out_shape=jax.ShapeDtypeStruct((tiles, r, r), F32),
        scratch_shapes=[pltpu.VMEM((tiles, r, 2 * r), F32)],
        compiler_params=pltpu.CompilerParams(vmem_limit_bytes=VMEM_LIMIT),
    )(total)
    summed = reduce_inner(ni, image.reshape(ni // 2, 2, tiles * r, share), False)
    summed = summed.reshape(tiles, r, share)
    mine = lax.dynamic_slice_in_dim(total, lax.axis_index("inner") * share, share, 2)
    basis = jnp.einsum("tde,tei->tdi", inverse, mine, precision=HIGHEST)
    image_out = jnp.einsum("tde,tei->tdi", inverse, summed, precision=HIGHEST)
    return (basis * math.sqrt(order), image_out)


def solution(mesh):
    return jax.shard_map(
        functools.partial(per_device, mesh.shape["tgt"], mesh.shape["inner"]),
        mesh=mesh,
        in_specs=(
            P(("tgt", "inner"), None, None),
            P(("tgt", "inner")),
            P(("tgt", "inner")),
            P(("tgt", "inner")),
            P(("tgt", "inner"), None, None),
            P(("tgt", "inner"), None, None),
            P(("tgt", "inner")),
            P(("tgt", "inner")),
            P(("tgt", "inner"), None, None),
            P(("tgt", "inner"), None, None),
            P("tgt"),
        ),
        out_specs=(P("tgt", None, "inner"), P("tgt", None, "inner")),
        check_vma=False,
    )
```

```python
import functools
import math

import jax
import jax.numpy as jnp
from jax import lax
from jax.experimental import pallas as pl
from jax.experimental.pallas import tpu as pltpu
from jax.sharding import PartitionSpec as P

HIGHEST = lax.Precision.HIGHEST
MESH = pl.DeviceIdType.MESH
F32 = jnp.float32
BF16 = jnp.bfloat16
VMEM_LIMIT = 56 * 1024 * 1024


def nt_dot(a, b):
    return lax.dot_general(a, b, (((1,), (1,)), ((), ())), preferred_element_type=F32)


def nn_dot(a, b):
    return lax.dot_general(a, b, (((1,), (0,)), ((), ())), preferred_element_type=F32)


def split(x):
    hi = x.astype(BF16)
    return hi, (x - hi.astype(F32)).astype(BF16)


def probe_table(seeds, rank_size, order):
    shape = (seeds.shape[0], rank_size, order)
    chan = lax.broadcasted_iota(jnp.int32, shape, 1)
    place = lax.broadcasted_iota(jnp.int32, shape, 2)
    code = (
        seeds[:, None, None] * 9973
        + place * place * 7
        + place * chan * 131
        + chan * chan * 17
        + place * 7919
        + chan * 104729
    ) % 65521
    return ((code.astype(F32) - 32760.0) / 32768.0).astype(BF16)


def gather_kernel(nt, u_ref, v_ref, su_ref, sv_ref, send, recv, local):
    me = lax.axis_index("tgt")
    k = u_ref.shape[0]
    mine = pl.ds(me * k, k)
    lu = pltpu.make_async_copy(u_ref, su_ref.at[mine], local.at[0])
    lv = pltpu.make_async_copy(v_ref, sv_ref.at[mine], local.at[1])
    lu.start()
    lv.start()
    barrier = pltpu.get_barrier_semaphore()

    def push(src, dst, sem, to):
        copy = pltpu.make_async_remote_copy(
            src_ref=src,
            dst_ref=dst,
            send_sem=send.at[sem],
            recv_sem=recv.at[sem],
            device_id={"tgt": to},
            device_id_type=MESH,
        )
        copy.start()
        return copy

    copies = []
    if nt == 4:
        a = me + 1 - 2 * (me % 2)
        b = (me + 2) % 4
        for peer in (a, b):
            pl.semaphore_signal(barrier, inc=1, device_id={"tgt": peer}, device_id_type=MESH)
        pl.semaphore_wait(barrier, 2)
        ua = push(u_ref, su_ref.at[mine], 0, a)
        vb = push(v_ref, sv_ref.at[mine], 1, b)
        va = push(v_ref, sv_ref.at[mine], 2, a)
        ub = push(u_ref, su_ref.at[mine], 3, b)
        from_a = pl.ds(a * k, k)
        from_b = pl.ds(b * k, k)
        ua.wait_recv()
        fu = push(su_ref.at[from_a], su_ref.at[from_a], 4, b)
        vb.wait_recv()
        fv = push(sv_ref.at[from_b], sv_ref.at[from_b], 5, a)
        for c in (va, ub, fu, fv):
            c.wait_recv()
        copies = [ua, vb, va, ub, fu, fv]
    else:
        for d in range(1, nt):
            pl.semaphore_signal(
                barrier, inc=1, device_id={"tgt": (me + d) % nt}, device_id_type=MESH
            )
        pl.semaphore_wait(barrier, nt - 1)
        for d in range(1, nt):
            to = (me + d) % nt
            copies.append(push(u_ref, su_ref.at[mine], 2 * d - 2, to))
            copies.append(push(v_ref, sv_ref.at[mine], 2 * d - 1, to))
        for c in copies:
            c.wait_recv()
    for c in copies:
        c.wait_send()
    lu.wait()
    lv.wait()


def gather_tiles(nt, u, v):
    sems = 6 if nt == 4 else max(2 * nt - 2, 1)
    shape = jax.ShapeDtypeStruct((nt * u.shape[0],) + u.shape[1:], u.dtype)
    return pl.pallas_call(
        functools.partial(gather_kernel, nt),
        out_shape=(shape, shape),
        in_specs=[pl.BlockSpec(memory_space=pl.ANY)] * 2,
        out_specs=[pl.BlockSpec(memory_space=pl.ANY)] * 2,
        scratch_shapes=[
            pltpu.SemaphoreType.DMA((sems,)),
            pltpu.SemaphoreType.DMA((sems,)),
            pltpu.SemaphoreType.DMA((2,)),
        ],
        compiler_params=pltpu.CompilerParams(collective_id=0, has_side_effects=True),
    )(u, v)


def reduce_kernel(n, gather, x_ref, *refs):
    if gather:
        out_ref, half, cut, part, total, send, recv = refs
    else:
        out_ref, half, cut, part, send, recv = refs
    me = lax.axis_index("inner")
    m = n // 2
    z = me // 2
    core = me % 2
    other = 1 - core
    sib = z * 2 + other
    barrier = pltpu.get_barrier_semaphore()
    pl.semaphore_signal(barrier, inc=1, device_id={"inner": sib}, device_id_type=MESH)
    for d in range(1, m):
        peer = ((z + d) % m) * 2 + core
        pl.semaphore_signal(barrier, inc=1, device_id={"inner": peer}, device_id_type=MESH)
    pl.semaphore_wait(barrier, m)

    def push(src, dst, sem, to):
        copy = pltpu.make_async_remote_copy(
            src_ref=src,
            dst_ref=dst,
            send_sem=send.at[sem],
            recv_sem=recv.at[sem],
            device_id={"inner": to},
            device_id_type=MESH,
        )
        copy.start()
        return copy

    pairs = []
    for d in range(m):
        q = (z + 1 + d) % m
        pairs.append(push(x_ref.at[q, other], half.at[q], d, sib))
    sends = []
    for d in range(m):
        q = (z + 1 + d) % m
        pairs[d].wait_recv()
        if d < m - 1:
            cut[d] = (half[q] + x_ref[q, core]).astype(BF16)
            sends.append(push(cut.at[d], part.at[m - 2 - d], m + d, q * 2 + core))
    acc = half[z] + x_ref[z, core]
    for d in range(m - 1):
        sends[d].wait_recv()
        acc = acc + part[m - 2 - d].astype(F32)
    if gather:
        total[...] = acc.astype(BF16)
        out_ref[z, core] = acc.astype(BF16)
        outs = [push(total, out_ref.at[z, core], 2 * m - 1, sib)]
        away = []
        for d in range(m - 1):
            q = (z + 1 + d) % m
            away.append(push(total, out_ref.at[z, core], 2 * m + d, q * 2 + core))
        for d in range(m - 1):
            q = (z + 2 * m - 1 - d) % m
            away[d].wait_recv()
            outs.append(push(out_ref.at[q, core], out_ref.at[q, core], 3 * m - 1 + d, sib))
        for c in outs:
            c.wait_recv()
        sends = sends + outs + away
    else:
        out_ref[...] = acc
    for c in pairs + sends:
        c.wait_send()


def reduce_inner(n, x, gather):
    m = n // 2
    block = x.shape[2:]
    sems = 4 * m - 2 if gather else 2 * m - 1
    return pl.pallas_call(
        functools.partial(reduce_kernel, n, gather),
        out_shape=jax.ShapeDtypeStruct(x.shape, BF16) if gather else jax.ShapeDtypeStruct(block, F32),
        in_specs=[pl.BlockSpec(memory_space=pltpu.VMEM)],
        out_specs=pl.BlockSpec(memory_space=pltpu.VMEM),
        scratch_shapes=[
            pltpu.VMEM((m,) + block, F32),
            pltpu.VMEM((max(m - 1, 1),) + block, BF16),
            pltpu.VMEM((max(m - 1, 1),) + block, BF16),
        ]
        + ([pltpu.VMEM(block, BF16)] if gather else [])
        + [pltpu.SemaphoreType.DMA((sems,)), pltpu.SemaphoreType.DMA((sems,))],
        compiler_params=pltpu.CompilerParams(
            collective_id=1 if gather else 2, has_side_effects=True, vmem_limit_bytes=VMEM_LIMIT
        ),
    )(x)


def sketch_kernel(batch, slots, right, target, near_right, near_target, count, *refs):
    u_refs, v_refs = refs[:batch], refs[batch : 2 * batch]
    low_u_ref, low_v_ref, near_ref, nu_ref, nv_ref, probe_ref = refs[2 * batch : 2 * batch + 6]
    mix_ref, lh_ref, ll_ref, sk_ref = refs[2 * batch + 6 :]
    j = pl.program_id(0)

    @pl.when(j == 0)
    def _():
        sk_ref[...] = jnp.zeros_like(sk_ref)

    terms = []
    for o in range(batch):
        t = target[j * batch + o]
        mixing = nt_dot(low_v_ref[o], u_refs[o][0]).astype(BF16)
        mix_ref[o] = mixing
        zh, zl = split(nt_dot(probe_ref[t], v_refs[o][0]))
        qh, ql = split(nt_dot(zh, mixing) + nt_dot(zl, mixing))
        low_u = low_u_ref[o]
        terms.append((t, nn_dot(qh, low_u) + nn_dot(ql, low_u)))
    for t, y in terms:
        sk_ref[t] += y

    @pl.when(j < slots)
    def _():
        t = near_target[j]
        live = (j < count[0]).astype(F32)
        left = nt_dot(nu_ref[0], near_ref[0]) * live
        lh, ll = split(left)
        lh_ref[0] = lh
        ll_ref[0] = ll
        zh, zl = split(nt_dot(probe_ref[t], nv_ref[0]))
        sk_ref[t] += nn_dot(zh, lh) + nn_dot(zl, lh) + nn_dot(zh, ll)


def add_columns(im_ref, t, y):
    n, share = im_ref.shape[0], im_ref.shape[3]
    for p in range(n):
        im_ref[p, t] += y[:, p * share : (p + 1) * share]


def image_kernel(batch, slots, right, target, near_right, near_target, *refs):
    v_refs = refs[:batch]
    low_u_ref, mix_ref, lh_ref, ll_ref, nv_ref, sk_ref, im_ref = refs[batch:]
    j = pl.program_id(0)

    @pl.when(j == 0)
    def _():
        im_ref[...] = jnp.zeros_like(im_ref)

    terms = []
    for o in range(batch):
        t = target[j * batch + o]
        wh, wl = split(nt_dot(sk_ref[t], low_u_ref[o]))
        mixing = mix_ref[o]
        ph, pll = split(nn_dot(wh, mixing) + nn_dot(wl, mixing))
        v = v_refs[o][0]
        terms.append((t, nn_dot(ph, v) + nn_dot(pll, v)))
    for t, y in terms:
        add_columns(im_ref, t, y)

    @pl.when(j < slots)
    def _():
        t = near_target[j]
        sk = sk_ref[t]
        ph, pll = split(nt_dot(sk, lh_ref[0]) + nt_dot(sk, ll_ref[0]))
        v = nv_ref[0]
        add_columns(im_ref, t, nn_dot(ph, v) + nn_dot(pll, v))


def chol_inv_kernel(s_ref, out_ref, a_ref):
    tiles, r, _ = s_ref.shape
    row = lax.broadcasted_iota(jnp.int32, (r, r), 0)
    col = lax.broadcasted_iota(jnp.int32, (r, r), 1)
    eye = (row == col).astype(F32)
    for t in range(tiles):
        s = s_ref[t]
        a_ref[t, :, :r] = lax.dot_general(
            s, s, (((1,), (1,)), ((), ())), preferred_element_type=F32
        )
        a_ref[t, :, r:] = eye
    rows = [a_ref[:, 8 * b : 8 * b + 8, :] for b in range(r // 8)]
    sub = lax.broadcasted_iota(jnp.int32, (tiles, 8, 2 * r), 1)
    for k in range(r):
        b0, e = k // 8, k % 8
        pivot = rows[b0][:, e : e + 1, :]
        inv = 1.0 / pivot[:, :, k : k + 1]
        scaled = pivot * inv
        for b in range(b0, r // 8):
            step = rows[b][:, :, k : k + 1] * scaled
            if b == b0:
                step = jnp.where(sub > e, step, 0.0)
            rows[b] = rows[b] - step
    lane = lax.broadcasted_iota(jnp.int32, (tiles, 8, 2 * r), 2)
    for b in range(r // 8):
        diag = jnp.sum(jnp.where(lane == sub + 8 * b, rows[b], 0.0), axis=2, keepdims=True)
        out_ref[:, 8 * b : 8 * b + 8, :] = (rows[b] * lax.rsqrt(diag))[:, :, r:]


def whole(shape):
    zeros = (0,) * len(shape)
    return pl.BlockSpec(shape, lambda j, *s: zeros)


def at_right(shape, batch, o):
    return pl.BlockSpec((1,) + shape[1:], lambda j, right, *s: (right[j * batch + o], 0, 0))


def at_near(shape, slots):
    return pl.BlockSpec(
        (1,) + shape[1:],
        lambda j, right, target, near, *s: (near[jnp.minimum(j, slots - 1)], 0, 0),
    )


def near_step(shape):
    return pl.BlockSpec(
        (1,) + shape[1:], lambda j, *s: (jnp.minimum(j, shape[0] - 1), 0, 0)
    )


def per_step(batch, shape):
    return pl.BlockSpec((batch,) + shape[1:], lambda j, *s: (j,) + (0,) * (len(shape) - 1))


def run(kernel, scalars, steps, ins, specs, outs, out_specs):
    return pl.pallas_call(
        kernel,
        grid_spec=pltpu.PrefetchScalarGridSpec(
            num_scalar_prefetch=len(scalars), grid=(steps,), in_specs=specs, out_specs=out_specs
        ),
        out_shape=outs,
        compiler_params=pltpu.CompilerParams(vmem_limit_bytes=VMEM_LIMIT),
    )(*scalars, *ins)


def per_device(
    nt,
    ni,
    near_tiles,
    near_target,
    near_right,
    near_count,
    low_u,
    low_v,
    low_target,
    low_right,
    right_u,
    right_v,
    probe_seed,
):
    slots, order = near_tiles.shape[0], near_tiles.shape[1]
    lows, r = low_u.shape[0], low_u.shape[1]
    tiles = probe_seed.shape[0]
    share = order // ni
    batch = math.gcd(lows, 4)
    while lows // batch < slots:
        batch = batch // 2
    steps = lows // batch
    seg_u, seg_v = gather_tiles(nt, right_u, right_v)
    probe = probe_table(probe_seed, r, order)
    sk = jax.ShapeDtypeStruct((tiles, r, order), F32)
    left = jax.ShapeDtypeStruct((slots, r, order), BF16)
    mix = jax.ShapeDtypeStruct((lows, r, r), BF16)
    near_specs = [at_near(seg_v.shape, slots)]
    mixing, lh, ll, sketch = run(
        functools.partial(sketch_kernel, batch, slots),
        (low_right, low_target, near_right, near_target, near_count),
        steps,
        (seg_u,) * batch + (seg_v,) * batch + (low_u, low_v, near_tiles, seg_u, seg_v, probe),
        [at_right(seg_u.shape, batch, o) for o in range(batch)] * 2
        + [per_step(batch, low_u.shape), per_step(batch, low_v.shape)]
        + [near_step(near_tiles.shape)]
        + near_specs * 2
        + [whole(probe.shape)],
        (mix, left, left, sk),
        (per_step(batch, mix.shape), near_step(left.shape), near_step(left.shape), whole(sk.shape)),
    )
    rows = tiles * r // ni
    total = reduce_inner(ni, sketch.reshape(ni // 2, 2, rows, order), True)
    total = total.reshape(tiles, r, order)
    im = jax.ShapeDtypeStruct((ni, tiles, r, share), F32)
    image = run(
        functools.partial(image_kernel, batch, slots),
        (low_right, low_target, near_right, near_target),
        steps,
        (seg_v,) * batch + (low_u, mixing, lh, ll, seg_v, total),
        [at_right(seg_v.shape, batch, o) for o in range(batch)]
        + [per_step(batch, low_u.shape), per_step(batch, mixing.shape)]
        + [near_step(lh.shape), near_step(ll.shape)]
        + near_specs
        + [whole(total.shape)],
        im,
        whole(im.shape),
    )
    inverse = pl.pallas_call(
        chol_inv_kernel,
        out_shape=jax.ShapeDtypeStruct((tiles, r, r), F32),
        scratch_shapes=[pltpu.VMEM((tiles, r, 2 * r), F32)],
        compiler_params=pltpu.CompilerParams(vmem_limit_bytes=VMEM_LIMIT),
    )(total)
    summed = reduce_inner(ni, image.reshape(ni // 2, 2, tiles * r, share), False)
    summed = summed.reshape(tiles, r, share)
    mine = lax.dynamic_slice_in_dim(total, lax.axis_index("inner") * share, share, 2).astype(F32)
    basis = jnp.einsum("tde,tei->tdi", inverse, mine, precision=HIGHEST)
    image_out = jnp.einsum("tde,tei->tdi", inverse, summed, precision=HIGHEST)
    return (basis * math.sqrt(order), image_out)


def solution(mesh):
    return jax.shard_map(
        functools.partial(per_device, mesh.shape["tgt"], mesh.shape["inner"]),
        mesh=mesh,
        in_specs=(
            P(("tgt", "inner"), None, None),
            P(("tgt", "inner")),
            P(("tgt", "inner")),
            P(("tgt", "inner")),
            P(("tgt", "inner"), None, None),
            P(("tgt", "inner"), None, None),
            P(("tgt", "inner")),
            P(("tgt", "inner")),
            P(("tgt", "inner"), None, None),
            P(("tgt", "inner"), None, None),
            P("tgt"),
        ),
        out_specs=(P("tgt", None, "inner"), P("tgt", None, "inner")),
        check_vma=False,
    )
```

```python
import functools
import math

import jax
import jax.numpy as jnp
from jax import lax
from jax.experimental import pallas as pl
from jax.experimental.pallas import tpu as pltpu
from jax.sharding import PartitionSpec as P

HIGHEST = lax.Precision.HIGHEST
MESH = pl.DeviceIdType.MESH
F32 = jnp.float32
BF16 = jnp.bfloat16
VMEM_LIMIT = 56 * 1024 * 1024


def nt_dot(a, b):
    return lax.dot_general(a, b, (((1,), (1,)), ((), ())), preferred_element_type=F32)


def nn_dot(a, b):
    return lax.dot_general(a, b, (((1,), (0,)), ((), ())), preferred_element_type=F32)


def split(x):
    hi = x.astype(BF16)
    return hi, (x - hi.astype(F32)).astype(BF16)


def probe_table(seeds, rank_size, order):
    shape = (seeds.shape[0], rank_size, order)
    chan = lax.broadcasted_iota(jnp.int32, shape, 1)
    place = lax.broadcasted_iota(jnp.int32, shape, 2)
    code = (
        seeds[:, None, None] * 9973
        + place * place * 7
        + place * chan * 131
        + chan * chan * 17
        + place * 7919
        + chan * 104729
    ) % 65521
    return ((code.astype(F32) - 32760.0) / 32768.0).astype(BF16)


def gather_kernel(nt, batch, low_right, near_right, count, u_ref, v_ref, low_v_ref, near_ref, *refs):
    sv_ref, mix_ref, lh_ref, ll_ref, su, sv, low_v, near, send, recv, local, out_sem = refs
    me = lax.axis_index("tgt")
    k = u_ref.shape[0]
    h = k // 2
    mine = pl.ds(me * k, k)
    loads = [
        pltpu.make_async_copy(u_ref, su.at[mine], local.at[0]),
        pltpu.make_async_copy(v_ref, sv.at[mine], local.at[1]),
        pltpu.make_async_copy(low_v_ref, low_v, local.at[2]),
        pltpu.make_async_copy(near_ref, near, local.at[3]),
    ]
    for c in loads:
        c.start()
    barrier = pltpu.get_barrier_semaphore()

    def push(src, dst, sem, to):
        copy = pltpu.make_async_remote_copy(
            src_ref=src,
            dst_ref=dst,
            send_sem=send.at[sem],
            recv_sem=recv.at[sem],
            device_id={"tgt": to},
            device_id_type=MESH,
        )
        copy.start()
        return copy

    def mix():
        loads[2].wait()

        def body(i, carry):
            for o in range(batch):
                j = i * batch + o
                mix_ref[j] = nt_dot(low_v[j], su[low_right[j]]).astype(BF16)
            return carry

        lax.fori_loop(0, low_v.shape[0] // batch, body, 0)

    def lefts():
        loads[3].wait()

        def body(j, carry):
            live = (j < count[0]).astype(F32)
            hi, lo = split(nt_dot(su[near_right[j]], near[j]) * live)
            lh_ref[j] = hi
            ll_ref[j] = lo
            return carry

        lax.fori_loop(0, near.shape[0], body, 0)

    if nt == 4:
        a = me + 1 - 2 * (me % 2)
        b = (me + 2) % 4
        for peer in (a, b):
            pl.semaphore_signal(barrier, inc=1, device_id={"tgt": peer}, device_id_type=MESH)
        pl.semaphore_wait(barrier, 2)

        def own(src, dst, sem):
            low, high = pl.ds(0, h), pl.ds(h, k - h)
            at_low, at_high = pl.ds(me * k, h), pl.ds(me * k + h, k - h)
            return [
                push(src.at[low], dst.at[at_low], sem, a),
                push(src.at[high], dst.at[at_high], sem + 1, b),
                push(src.at[high], dst.at[at_high], sem + 2, a),
                push(src.at[low], dst.at[at_low], sem + 3, b),
            ]

        def onward(dst, copies, sem):
            from_a, from_b = pl.ds(a * k, h), pl.ds(b * k + h, k - h)
            copies[0].wait_recv()
            fa = push(dst.at[from_a], dst.at[from_a], sem, b)
            copies[1].wait_recv()
            return [fa, push(dst.at[from_b], dst.at[from_b], sem + 1, a)]

        us = own(u_ref, su, 0)
        uf = onward(su, us, 4)
        vs = own(v_ref, sv, 6)
        for c in us[2:] + uf:
            c.wait_recv()
        loads[0].wait()
        mix()
        vf = onward(sv, vs, 10)
        lefts()
        for c in vs[2:] + vf:
            c.wait_recv()
        copies = us + uf + vs + vf
    else:
        for d in range(1, nt):
            pl.semaphore_signal(
                barrier, inc=1, device_id={"tgt": (me + d) % nt}, device_id_type=MESH
            )
        pl.semaphore_wait(barrier, nt - 1)
        copies = []
        for d in range(1, nt):
            to = (me + d) % nt
            copies.append(push(u_ref, su.at[mine], 2 * d - 2, to))
            copies.append(push(v_ref, sv.at[mine], 2 * d - 1, to))
        for c in copies:
            c.wait_recv()
        loads[0].wait()
        mix()
        lefts()
    loads[1].wait()
    out = pltpu.make_async_copy(sv, sv_ref, out_sem)
    out.start()
    for c in copies:
        c.wait_send()
    out.wait()


def gather_tiles(nt, batch, low_right, near_right, count, u, v, low_v, near):
    sems = 12 if nt == 4 else max(2 * nt - 2, 1)
    seg = (nt * u.shape[0],) + u.shape[1:]
    r = u.shape[1]
    left = jax.ShapeDtypeStruct((near.shape[0], r, near.shape[1]), BF16)
    return pl.pallas_call(
        functools.partial(gather_kernel, nt, batch),
        out_shape=(
            jax.ShapeDtypeStruct(seg, v.dtype),
            jax.ShapeDtypeStruct((low_v.shape[0], low_v.shape[1], r), BF16),
            left,
            left,
        ),
        in_specs=[pl.BlockSpec(memory_space=pltpu.SMEM)] * 3
        + [pl.BlockSpec(memory_space=pl.ANY)] * 4,
        out_specs=[pl.BlockSpec(memory_space=pl.ANY)]
        + [pl.BlockSpec(memory_space=pltpu.VMEM)] * 3,
        scratch_shapes=[
            pltpu.VMEM(seg, u.dtype),
            pltpu.VMEM(seg, v.dtype),
            pltpu.VMEM(low_v.shape, low_v.dtype),
            pltpu.VMEM(near.shape, near.dtype),
            pltpu.SemaphoreType.DMA((sems,)),
            pltpu.SemaphoreType.DMA((sems,)),
            pltpu.SemaphoreType.DMA((4,)),
            pltpu.SemaphoreType.DMA,
        ],
        compiler_params=pltpu.CompilerParams(
            collective_id=0, has_side_effects=True, vmem_limit_bytes=VMEM_LIMIT
        ),
    )(low_right, near_right, count, u, v, low_v, near)


def chol_inverse(s_ref, out_ref, a_ref):
    tiles, r, _ = s_ref.shape
    row = lax.broadcasted_iota(jnp.int32, (r, r), 0)
    col = lax.broadcasted_iota(jnp.int32, (r, r), 1)
    eye = (row == col).astype(F32)
    for t in range(tiles):
        s = s_ref[t]
        a_ref[t, :, :r] = nt_dot(s, s)
        a_ref[t, :, r:] = eye
    for base in range(0, r, 8):
        shape = (tiles, r - base, 2 * r)
        sub = lax.broadcasted_iota(jnp.int32, shape, 1) + base
        lane = lax.broadcasted_iota(jnp.int32, shape, 2)

        def body(k, carry):
            whole_a = a_ref[:, base:, :]
            pivot = a_ref[:, pl.ds(k, 1), :]
            column = jnp.sum(jnp.where(lane == k, whole_a, 0.0), axis=2, keepdims=True)
            diag = jnp.sum(jnp.where(lane[:, :1] == k, pivot, 0.0), axis=2, keepdims=True)
            step = column * (pivot / diag)
            a_ref[:, base:, :] = whole_a - jnp.where(sub > k, step, 0.0)
            return carry

        lax.fori_loop(base, base + 8, body, 0)
    a = a_ref[...]
    sub = lax.broadcasted_iota(jnp.int32, a.shape, 1)
    lane = lax.broadcasted_iota(jnp.int32, a.shape, 2)
    diag = jnp.sum(jnp.where(lane == sub, a, 0.0), axis=2, keepdims=True)
    out_ref[...] = (a * lax.rsqrt(diag))[:, :, r:]


def reduce_kernel(n, gather, x_ref, *refs):
    if gather:
        out_ref, half, cut, part, total, send, recv = refs
    else:
        s_ref, out_ref, inv_ref, half, cut, part, a_ref, send, recv = refs
    me = lax.axis_index("inner")
    m = n // 2
    z = me // 2
    core = me % 2
    other = 1 - core
    sib = z * 2 + other
    barrier = pltpu.get_barrier_semaphore()
    pl.semaphore_signal(barrier, inc=1, device_id={"inner": sib}, device_id_type=MESH)
    for d in range(1, m):
        peer = ((z + d) % m) * 2 + core
        pl.semaphore_signal(barrier, inc=1, device_id={"inner": peer}, device_id_type=MESH)
    pl.semaphore_wait(barrier, m)

    def push(src, dst, sem, to):
        copy = pltpu.make_async_remote_copy(
            src_ref=src,
            dst_ref=dst,
            send_sem=send.at[sem],
            recv_sem=recv.at[sem],
            device_id={"inner": to},
            device_id_type=MESH,
        )
        copy.start()
        return copy

    pairs = []
    for d in range(m):
        q = (z + 1 + d) % m
        pairs.append(push(x_ref.at[q, other], half.at[q], d, sib))
    sends = []
    for d in range(m):
        q = (z + 1 + d) % m
        pairs[d].wait_recv()
        if d < m - 1:
            cut[d] = (half[q] + x_ref[q, core]).astype(BF16)
            sends.append(push(cut.at[d], part.at[m - 2 - d], m + d, q * 2 + core))
    if not gather:
        chol_inverse(s_ref, inv_ref, a_ref)
    acc = half[z] + x_ref[z, core]
    for d in range(m - 1):
        sends[d].wait_recv()
        acc = acc + part[m - 2 - d].astype(F32)
    if gather:
        total[...] = acc.astype(BF16)
        out_ref[z, core] = acc.astype(BF16)
        outs = [push(total, out_ref.at[z, core], 2 * m - 1, sib)]
        away = []
        for d in range(m - 1):
            q = (z + 1 + d) % m
            away.append(push(total, out_ref.at[z, core], 2 * m + d, q * 2 + core))
        for d in range(m - 1):
            q = (z + 2 * m - 1 - d) % m
            away[d].wait_recv()
            outs.append(push(out_ref.at[q, core], out_ref.at[q, core], 3 * m - 1 + d, sib))
        for c in outs:
            c.wait_recv()
        sends = sends + outs + away
    else:
        out_ref[...] = acc
    for c in pairs + sends:
        c.wait_send()


def reduce_inner(n, x, gather, sketch=None):
    m = n // 2
    block = x.shape[2:]
    sems = 4 * m - 2 if gather else 2 * m - 1
    args = [x] if gather else [x, sketch]
    scratch = [pltpu.VMEM((m,) + block, F32)] + [pltpu.VMEM((max(m - 1, 1),) + block, BF16)] * 2
    vmem = pl.BlockSpec(memory_space=pltpu.VMEM)
    if gather:
        outs, specs = jax.ShapeDtypeStruct(x.shape, BF16), vmem
        scratch.append(pltpu.VMEM(block, BF16))
    else:
        tiles, r, _ = sketch.shape
        outs = (jax.ShapeDtypeStruct(block, F32), jax.ShapeDtypeStruct((tiles, r, r), F32))
        specs = (vmem, vmem)
        scratch.append(pltpu.VMEM((tiles, r, 2 * r), F32))
    return pl.pallas_call(
        functools.partial(reduce_kernel, n, gather),
        out_shape=outs,
        in_specs=[vmem] * len(args),
        out_specs=specs,
        scratch_shapes=scratch + [pltpu.SemaphoreType.DMA((sems,))] * 2,
        compiler_params=pltpu.CompilerParams(
            collective_id=1 if gather else 2, has_side_effects=True, vmem_limit_bytes=VMEM_LIMIT
        ),
    )(*args)


def sketch_kernel(batch, slots, right, target, near_right, near_target, *refs):
    v_refs = refs[:batch]
    low_u_ref, mix_ref, lh_ref, ll_ref, nv_ref, probe_ref, sk_ref = refs[batch:]
    j = pl.program_id(0)

    @pl.when(j == 0)
    def _():
        sk_ref[...] = jnp.zeros_like(sk_ref)

    terms = []
    for o in range(batch):
        t = target[j * batch + o]
        mixing = mix_ref[o]
        zh, zl = split(nt_dot(probe_ref[t], v_refs[o][0]))
        qh, ql = split(nt_dot(zh, mixing) + nt_dot(zl, mixing))
        low_u = low_u_ref[o]
        terms.append((t, nn_dot(qh, low_u) + nn_dot(ql, low_u)))
    for t, y in terms:
        sk_ref[t] += y

    @pl.when(j < slots)
    def _():
        t = near_target[j]
        lh = lh_ref[0]
        zh, zl = split(nt_dot(probe_ref[t], nv_ref[0]))
        sk_ref[t] += nn_dot(zh, lh) + nn_dot(zl, lh) + nn_dot(zh, ll_ref[0])


def add_columns(im_ref, t, y):
    n, share = im_ref.shape[0], im_ref.shape[3]
    for p in range(n):
        im_ref[p, t] += y[:, p * share : (p + 1) * share]


def image_kernel(batch, slots, right, target, near_right, near_target, *refs):
    v_refs = refs[:batch]
    low_u_ref, mix_ref, lh_ref, ll_ref, nv_ref, sk_ref, im_ref = refs[batch:]
    j = pl.program_id(0)

    @pl.when(j == 0)
    def _():
        im_ref[...] = jnp.zeros_like(im_ref)

    terms = []
    for o in range(batch):
        t = target[j * batch + o]
        wh, wl = split(nt_dot(sk_ref[t], low_u_ref[o]))
        mixing = mix_ref[o]
        ph, pll = split(nn_dot(wh, mixing) + nn_dot(wl, mixing))
        v = v_refs[o][0]
        terms.append((t, nn_dot(ph, v) + nn_dot(pll, v)))
    for t, y in terms:
        add_columns(im_ref, t, y)

    @pl.when(j < slots)
    def _():
        t = near_target[j]
        sk = sk_ref[t]
        ph, pll = split(nt_dot(sk, lh_ref[0]) + nt_dot(sk, ll_ref[0]))
        v = nv_ref[0]
        add_columns(im_ref, t, nn_dot(ph, v) + nn_dot(pll, v))


def whole(shape):
    zeros = (0,) * len(shape)
    return pl.BlockSpec(shape, lambda j, *s: zeros)


def at_right(shape, batch, o):
    return pl.BlockSpec((1,) + shape[1:], lambda j, right, *s: (right[j * batch + o], 0, 0))


def at_near(shape, slots):
    return pl.BlockSpec(
        (1,) + shape[1:],
        lambda j, right, target, near, *s: (near[jnp.minimum(j, slots - 1)], 0, 0),
    )


def near_step(shape):
    return pl.BlockSpec(
        (1,) + shape[1:], lambda j, *s: (jnp.minimum(j, shape[0] - 1), 0, 0)
    )


def per_step(batch, shape):
    return pl.BlockSpec((batch,) + shape[1:], lambda j, *s: (j,) + (0,) * (len(shape) - 1))


def run(kernel, scalars, steps, ins, specs, outs, out_specs):
    return pl.pallas_call(
        kernel,
        grid_spec=pltpu.PrefetchScalarGridSpec(
            num_scalar_prefetch=len(scalars), grid=(steps,), in_specs=specs, out_specs=out_specs
        ),
        out_shape=outs,
        compiler_params=pltpu.CompilerParams(vmem_limit_bytes=VMEM_LIMIT),
    )(*scalars, *ins)


def per_device(
    nt,
    ni,
    near_tiles,
    near_target,
    near_right,
    near_count,
    low_u,
    low_v,
    low_target,
    low_right,
    right_u,
    right_v,
    probe_seed,
):
    slots, order = near_tiles.shape[0], near_tiles.shape[1]
    lows, r = low_u.shape[0], low_u.shape[1]
    tiles = probe_seed.shape[0]
    share = order // ni
    batch = math.gcd(lows, 4)
    while lows // batch < slots:
        batch = batch // 2
    steps = lows // batch
    seg_v, mixing, lh, ll = gather_tiles(
        nt, batch, low_right, near_right, near_count, right_u, right_v, low_v, near_tiles
    )
    probe = probe_table(probe_seed, r, order)
    sk = jax.ShapeDtypeStruct((tiles, r, order), F32)
    near_specs = [at_near(seg_v.shape, slots)]
    pair_specs = (
        [at_right(seg_v.shape, batch, o) for o in range(batch)]
        + [per_step(batch, low_u.shape), per_step(batch, mixing.shape)]
        + [near_step(lh.shape), near_step(ll.shape)]
        + near_specs
    )
    scalars = (low_right, low_target, near_right, near_target)
    pair_args = (seg_v,) * batch + (low_u, mixing, lh, ll, seg_v)
    sketch = run(
        functools.partial(sketch_kernel, batch, slots),
        scalars,
        steps,
        pair_args + (probe,),
        pair_specs + [whole(probe.shape)],
        sk,
        whole(sk.shape),
    )
    rows = tiles * r // ni
    total = reduce_inner(ni, sketch.reshape(ni // 2, 2, rows, order), True)
    total = total.reshape(tiles, r, order)
    im = jax.ShapeDtypeStruct((ni, tiles, r, share), F32)
    image = run(
        functools.partial(image_kernel, batch, slots),
        scalars,
        steps,
        pair_args + (total,),
        pair_specs + [whole(total.shape)],
        im,
        whole(im.shape),
    )
    summed, inverse = reduce_inner(
        ni, image.reshape(ni // 2, 2, tiles * r, share), False, total
    )
    summed = summed.reshape(tiles, r, share)
    mine = lax.dynamic_slice_in_dim(total, lax.axis_index("inner") * share, share, 2).astype(F32)
    basis = jnp.einsum("tde,tei->tdi", inverse, mine, precision=HIGHEST)
    image_out = jnp.einsum("tde,tei->tdi", inverse, summed, precision=HIGHEST)
    return (basis * math.sqrt(order), image_out)


def solution(mesh):
    return jax.shard_map(
        functools.partial(per_device, mesh.shape["tgt"], mesh.shape["inner"]),
        mesh=mesh,
        in_specs=(
            P(("tgt", "inner"), None, None),
            P(("tgt", "inner")),
            P(("tgt", "inner")),
            P(("tgt", "inner")),
            P(("tgt", "inner"), None, None),
            P(("tgt", "inner"), None, None),
            P(("tgt", "inner")),
            P(("tgt", "inner")),
            P(("tgt", "inner"), None, None),
            P(("tgt", "inner"), None, None),
            P("tgt"),
        ),
        out_specs=(P("tgt", None, "inner"), P("tgt", None, "inner")),
        check_vma=False,
    )
```

```python
import functools
import math

import jax
import jax.numpy as jnp
from jax import lax
from jax.experimental import pallas as pl
from jax.experimental.pallas import tpu as pltpu
from jax.sharding import PartitionSpec as P

HIGHEST = lax.Precision.HIGHEST
MESH = pl.DeviceIdType.MESH
F32 = jnp.float32
BF16 = jnp.bfloat16
VMEM_LIMIT = 56 * 1024 * 1024


def nt_dot(a, b):
    return lax.dot_general(a, b, (((1,), (1,)), ((), ())), preferred_element_type=F32)


def nn_dot(a, b):
    return lax.dot_general(a, b, (((1,), (0,)), ((), ())), preferred_element_type=F32)


def split(x):
    hi = x.astype(BF16)
    return hi, (x - hi.astype(F32)).astype(BF16)


def probe_table(seeds, rank_size, order):
    shape = (seeds.shape[0], rank_size, order)
    chan = lax.broadcasted_iota(jnp.int32, shape, 1)
    place = lax.broadcasted_iota(jnp.int32, shape, 2)
    code = (
        seeds[:, None, None] * 9973
        + place * place * 7
        + place * chan * 131
        + chan * chan * 17
        + place * 7919
        + chan * 104729
    ) % 65521
    return ((code.astype(F32) - 32760.0) / 32768.0).astype(BF16)


def gather_kernel(nt, batch, low_right, near_right, count, u_ref, v_ref, low_v_ref, near_ref, *refs):
    sv_ref, mix_ref, lh_ref, ll_ref, su, sv, low_v, near, send, recv, local, out_sem = refs
    me = lax.axis_index("tgt")
    k = u_ref.shape[0]
    h = k // 2
    mine = pl.ds(me * k, k)
    loads = [
        pltpu.make_async_copy(u_ref, su.at[mine], local.at[0]),
        pltpu.make_async_copy(v_ref, sv.at[mine], local.at[1]),
        pltpu.make_async_copy(low_v_ref, low_v, local.at[2]),
        pltpu.make_async_copy(near_ref, near, local.at[3]),
    ]
    for c in loads:
        c.start()
    barrier = pltpu.get_barrier_semaphore()

    def push(src, dst, sem, to):
        copy = pltpu.make_async_remote_copy(
            src_ref=src,
            dst_ref=dst,
            send_sem=send.at[sem],
            recv_sem=recv.at[sem],
            device_id={"tgt": to},
            device_id_type=MESH,
        )
        copy.start()
        return copy

    def mix():
        loads[2].wait()

        def body(i, carry):
            for o in range(batch):
                j = i * batch + o
                mix_ref[j] = nt_dot(low_v[j], su[low_right[j]]).astype(BF16)
            return carry

        lax.fori_loop(0, low_v.shape[0] // batch, body, 0)

    def lefts():
        loads[3].wait()

        def body(j, carry):
            live = (j < count[0]).astype(F32)
            hi, lo = split(nt_dot(su[near_right[j]], near[j]) * live)
            lh_ref[j] = hi
            ll_ref[j] = lo
            return carry

        lax.fori_loop(0, near.shape[0], body, 0)

    if nt == 4:
        a = me + 1 - 2 * (me % 2)
        b = (me + 2) % 4
        for peer in (a, b):
            pl.semaphore_signal(barrier, inc=1, device_id={"tgt": peer}, device_id_type=MESH)
        pl.semaphore_wait(barrier, 2)

        def own(src, dst, sem):
            low, high = pl.ds(0, h), pl.ds(h, k - h)
            at_low, at_high = pl.ds(me * k, h), pl.ds(me * k + h, k - h)
            return [
                push(src.at[low], dst.at[at_low], sem, a),
                push(src.at[high], dst.at[at_high], sem + 1, b),
                push(src.at[high], dst.at[at_high], sem + 2, a),
                push(src.at[low], dst.at[at_low], sem + 3, b),
            ]

        def onward(dst, copies, sem):
            from_a, from_b = pl.ds(a * k, h), pl.ds(b * k + h, k - h)
            copies[0].wait_recv()
            fa = push(dst.at[from_a], dst.at[from_a], sem, b)
            copies[1].wait_recv()
            return [fa, push(dst.at[from_b], dst.at[from_b], sem + 1, a)]

        us = own(u_ref, su, 0)
        uf = onward(su, us, 4)
        vs = own(v_ref, sv, 6)
        for c in us[2:] + uf:
            c.wait_recv()
        loads[0].wait()
        mix()
        vf = onward(sv, vs, 10)
        lefts()
        for c in vs[2:] + vf:
            c.wait_recv()
        copies = us + uf + vs + vf
    else:
        for d in range(1, nt):
            pl.semaphore_signal(
                barrier, inc=1, device_id={"tgt": (me + d) % nt}, device_id_type=MESH
            )
        pl.semaphore_wait(barrier, nt - 1)
        copies = []
        for d in range(1, nt):
            to = (me + d) % nt
            copies.append(push(u_ref, su.at[mine], 2 * d - 2, to))
            copies.append(push(v_ref, sv.at[mine], 2 * d - 1, to))
        for c in copies:
            c.wait_recv()
        loads[0].wait()
        mix()
        lefts()
    loads[1].wait()
    out = pltpu.make_async_copy(sv, sv_ref, out_sem)
    out.start()
    for c in copies:
        c.wait_send()
    out.wait()


def gather_tiles(nt, batch, low_right, near_right, count, u, v, low_v, near):
    sems = 12 if nt == 4 else max(2 * nt - 2, 1)
    seg = (nt * u.shape[0],) + u.shape[1:]
    r = u.shape[1]
    left = jax.ShapeDtypeStruct((near.shape[0], r, near.shape[1]), BF16)
    return pl.pallas_call(
        functools.partial(gather_kernel, nt, batch),
        out_shape=(
            jax.ShapeDtypeStruct(seg, v.dtype),
            jax.ShapeDtypeStruct((low_v.shape[0], low_v.shape[1], r), BF16),
            left,
            left,
        ),
        in_specs=[pl.BlockSpec(memory_space=pltpu.SMEM)] * 3
        + [pl.BlockSpec(memory_space=pl.ANY)] * 4,
        out_specs=[pl.BlockSpec(memory_space=pl.ANY)]
        + [pl.BlockSpec(memory_space=pltpu.VMEM)] * 3,
        scratch_shapes=[
            pltpu.VMEM(seg, u.dtype),
            pltpu.VMEM(seg, v.dtype),
            pltpu.VMEM(low_v.shape, low_v.dtype),
            pltpu.VMEM(near.shape, near.dtype),
            pltpu.SemaphoreType.DMA((sems,)),
            pltpu.SemaphoreType.DMA((sems,)),
            pltpu.SemaphoreType.DMA((4,)),
            pltpu.SemaphoreType.DMA,
        ],
        compiler_params=pltpu.CompilerParams(
            collective_id=0, has_side_effects=True, vmem_limit_bytes=VMEM_LIMIT
        ),
    )(low_right, near_right, count, u, v, low_v, near)


def chol_inverse(s_ref, out_ref, a_ref):
    tiles, r, _ = s_ref.shape
    row = lax.broadcasted_iota(jnp.int32, (r, r), 0)
    col = lax.broadcasted_iota(jnp.int32, (r, r), 1)
    eye = (row == col).astype(F32)
    for t in range(tiles):
        s = s_ref[t]
        a_ref[t, :, :r] = nt_dot(s, s)
        a_ref[t, :, r:] = eye
    for base in range(0, r, 8):
        shape = (tiles, r - base, 2 * r)
        sub = lax.broadcasted_iota(jnp.int32, shape, 1) + base
        lane = lax.broadcasted_iota(jnp.int32, shape, 2)

        def body(k, carry):
            whole_a = a_ref[:, base:, :]
            pivot = a_ref[:, pl.ds(k, 1), :]
            column = jnp.sum(jnp.where(lane == k, whole_a, 0.0), axis=2, keepdims=True)
            diag = jnp.sum(jnp.where(lane[:, :1] == k, pivot, 0.0), axis=2, keepdims=True)
            step = column * (pivot / diag)
            a_ref[:, base:, :] = whole_a - jnp.where(sub > k, step, 0.0)
            return carry

        lax.fori_loop(base, base + 8, body, 0)
    a = a_ref[...]
    sub = lax.broadcasted_iota(jnp.int32, a.shape, 1)
    lane = lax.broadcasted_iota(jnp.int32, a.shape, 2)
    diag = jnp.sum(jnp.where(lane == sub, a, 0.0), axis=2, keepdims=True)
    out_ref[...] = (a * lax.rsqrt(diag))[:, :, r:]


def reduce_kernel(n, gather, x_ref, *refs):
    if gather:
        out_ref, half, cut, part, total, send, recv = refs
    else:
        s_ref, out_ref, inv_ref, half, cut, part, a_ref, send, recv = refs
    me = lax.axis_index("inner")
    m = n // 2
    z = me // 2
    core = me % 2
    other = 1 - core
    sib = z * 2 + other
    barrier = pltpu.get_barrier_semaphore()
    pl.semaphore_signal(barrier, inc=1, device_id={"inner": sib}, device_id_type=MESH)
    for d in range(1, m):
        peer = ((z + d) % m) * 2 + core
        pl.semaphore_signal(barrier, inc=1, device_id={"inner": peer}, device_id_type=MESH)
    pl.semaphore_wait(barrier, m)

    def push(src, dst, sem, to):
        copy = pltpu.make_async_remote_copy(
            src_ref=src,
            dst_ref=dst,
            send_sem=send.at[sem],
            recv_sem=recv.at[sem],
            device_id={"inner": to},
            device_id_type=MESH,
        )
        copy.start()
        return copy

    pairs = []
    for d in range(m):
        q = (z + 1 + d) % m
        pairs.append(push(x_ref.at[q, other], half.at[q], d, sib))
    sends = []
    for d in range(m):
        q = (z + 1 + d) % m
        pairs[d].wait_recv()
        if d < m - 1:
            cut[d] = (half[q] + x_ref[q, core]).astype(BF16)
            sends.append(push(cut.at[d], part.at[m - 2 - d], m + d, q * 2 + core))
    if not gather:
        chol_inverse(s_ref, inv_ref, a_ref)
    acc = half[z] + x_ref[z, core]
    for d in range(m - 1):
        sends[d].wait_recv()
        acc = acc + part[m - 2 - d].astype(F32)
    if gather:
        total[...] = acc.astype(BF16)
        out_ref[z, core] = acc.astype(BF16)
        outs = [push(total, out_ref.at[z, core], 2 * m - 1, sib)]
        away = []
        for d in range(m - 1):
            q = (z + 1 + d) % m
            away.append(push(total, out_ref.at[z, core], 2 * m + d, q * 2 + core))
        for d in range(m - 1):
            q = (z + 2 * m - 1 - d) % m
            away[d].wait_recv()
            outs.append(push(out_ref.at[q, core], out_ref.at[q, core], 3 * m - 1 + d, sib))
        for c in outs:
            c.wait_recv()
        sends = sends + outs + away
    else:
        out_ref[...] = acc
    for c in pairs + sends:
        c.wait_send()


def reduce_inner(n, x, gather, sketch=None):
    m = n // 2
    block = x.shape[2:]
    sems = 4 * m - 2 if gather else 2 * m - 1
    args = [x] if gather else [x, sketch]
    scratch = [pltpu.VMEM((m,) + block, F32)] + [pltpu.VMEM((max(m - 1, 1),) + block, BF16)] * 2
    vmem = pl.BlockSpec(memory_space=pltpu.VMEM)
    if gather:
        outs, specs = jax.ShapeDtypeStruct(x.shape, BF16), vmem
        scratch.append(pltpu.VMEM(block, BF16))
    else:
        tiles, r, _ = sketch.shape
        outs = (jax.ShapeDtypeStruct(block, F32), jax.ShapeDtypeStruct((tiles, r, r), F32))
        specs = (vmem, vmem)
        scratch.append(pltpu.VMEM((tiles, r, 2 * r), F32))
    return pl.pallas_call(
        functools.partial(reduce_kernel, n, gather),
        out_shape=outs,
        in_specs=[vmem] * len(args),
        out_specs=specs,
        scratch_shapes=scratch + [pltpu.SemaphoreType.DMA((sems,))] * 2,
        compiler_params=pltpu.CompilerParams(
            collective_id=1 if gather else 2, has_side_effects=True, vmem_limit_bytes=VMEM_LIMIT
        ),
    )(*args)


def both(x, axis):
    return jnp.concatenate([x, x], axis=axis)


def parts(x):
    return jnp.concatenate(split(x), axis=1)


def sketch_kernel(batch, slots, steps, right, target, near_right, near_target, *refs):
    v_refs = refs[:batch]
    low_u_ref, mix_ref, lh_ref, ll_ref, nv_ref, probe_ref, sk_ref = refs[batch:]
    j = pl.program_id(0)

    @pl.when(j == 0)
    def _():
        sk_ref[...] = jnp.zeros_like(sk_ref)

    def near_term():
        t = near_target[j]
        lh = lh_ref[0]
        zh, zl = split(nt_dot(probe_ref[t], nv_ref[0]))
        left = jnp.concatenate([lh, lh, ll_ref[0]], axis=0)
        sk_ref[t] += nn_dot(jnp.concatenate([zh, zl, zh], axis=1), left)

    span = range(batch)
    where = [target[j * batch + o] for o in span]
    zeta = [nt_dot(probe_ref[where[o]], v_refs[o][0]) for o in span]
    zeta = [parts(x) for x in zeta]
    q = [nt_dot(zeta[o], both(mix_ref[o], 1)) for o in span]
    q = [parts(x) for x in q]
    for o in span:
        sk_ref[where[o]] += nn_dot(q[o], both(low_u_ref[o], 0))
    if slots == steps:
        near_term()
    else:
        pl.when(j < slots)(near_term)


def add_columns(im_ref, t, y):
    n, share = im_ref.shape[0], im_ref.shape[3]
    for p in range(n):
        im_ref[p, t] += y[:, p * share : (p + 1) * share]


def image_kernel(batch, slots, steps, right, target, near_right, near_target, *refs):
    v_refs = refs[:batch]
    low_u_ref, mix_ref, lh_ref, ll_ref, nv_ref, sk_ref, im_ref = refs[batch:]
    j = pl.program_id(0)

    @pl.when(j == 0)
    def _():
        im_ref[...] = jnp.zeros_like(im_ref)

    def near_term():
        t = near_target[j]
        left = jnp.concatenate([lh_ref[0], ll_ref[0]], axis=1)
        proj = nt_dot(both(sk_ref[t], 1), left)
        add_columns(im_ref, t, nn_dot(parts(proj), both(nv_ref[0], 0)))

    span = range(batch)
    where = [target[j * batch + o] for o in span]
    w = [nt_dot(sk_ref[where[o]], low_u_ref[o]) for o in span]
    w = [parts(x) for x in w]
    proj = [nn_dot(w[o], both(mix_ref[o], 0)) for o in span]
    proj = [parts(x) for x in proj]
    for o in span:
        add_columns(im_ref, where[o], nn_dot(proj[o], both(v_refs[o][0], 0)))
    if slots == steps:
        near_term()
    else:
        pl.when(j < slots)(near_term)


def whole(shape):
    zeros = (0,) * len(shape)
    return pl.BlockSpec(shape, lambda j, *s: zeros)


def at_right(shape, batch, o):
    return pl.BlockSpec((1,) + shape[1:], lambda j, right, *s: (right[j * batch + o], 0, 0))


def at_near(shape, slots):
    return pl.BlockSpec(
        (1,) + shape[1:],
        lambda j, right, target, near, *s: (near[jnp.minimum(j, slots - 1)], 0, 0),
    )


def near_step(shape):
    return pl.BlockSpec(
        (1,) + shape[1:], lambda j, *s: (jnp.minimum(j, shape[0] - 1), 0, 0)
    )


def per_step(batch, shape):
    return pl.BlockSpec((batch,) + shape[1:], lambda j, *s: (j,) + (0,) * (len(shape) - 1))


def run(kernel, scalars, steps, ins, specs, outs, out_specs):
    return pl.pallas_call(
        kernel,
        grid_spec=pltpu.PrefetchScalarGridSpec(
            num_scalar_prefetch=len(scalars), grid=(steps,), in_specs=specs, out_specs=out_specs
        ),
        out_shape=outs,
        compiler_params=pltpu.CompilerParams(vmem_limit_bytes=VMEM_LIMIT),
    )(*scalars, *ins)


def per_device(
    nt,
    ni,
    near_tiles,
    near_target,
    near_right,
    near_count,
    low_u,
    low_v,
    low_target,
    low_right,
    right_u,
    right_v,
    probe_seed,
):
    slots, order = near_tiles.shape[0], near_tiles.shape[1]
    lows, r = low_u.shape[0], low_u.shape[1]
    tiles = probe_seed.shape[0]
    share = order // ni
    batch = math.gcd(lows, 8)
    while lows // batch < slots:
        batch = batch // 2
    steps = lows // batch
    seg_v, mixing, lh, ll = gather_tiles(
        nt, batch, low_right, near_right, near_count, right_u, right_v, low_v, near_tiles
    )
    probe = probe_table(probe_seed, r, order)
    sk = jax.ShapeDtypeStruct((tiles, r, order), F32)
    near_specs = [at_near(seg_v.shape, slots)]
    pair_specs = (
        [at_right(seg_v.shape, batch, o) for o in range(batch)]
        + [per_step(batch, low_u.shape), per_step(batch, mixing.shape)]
        + [near_step(lh.shape), near_step(ll.shape)]
        + near_specs
    )
    scalars = (low_right, low_target, near_right, near_target)
    pair_args = (seg_v,) * batch + (low_u, mixing, lh, ll, seg_v)
    sketch = run(
        functools.partial(sketch_kernel, batch, slots, steps),
        scalars,
        steps,
        pair_args + (probe,),
        pair_specs + [whole(probe.shape)],
        sk,
        whole(sk.shape),
    )
    rows = tiles * r // ni
    total = reduce_inner(ni, sketch.reshape(ni // 2, 2, rows, order), True)
    total = total.reshape(tiles, r, order)
    im = jax.ShapeDtypeStruct((ni, tiles, r, share), F32)
    image = run(
        functools.partial(image_kernel, batch, slots, steps),
        scalars,
        steps,
        pair_args + (total,),
        pair_specs + [whole(total.shape)],
        im,
        whole(im.shape),
    )
    summed, inverse = reduce_inner(
        ni, image.reshape(ni // 2, 2, tiles * r, share), False, total
    )
    summed = summed.reshape(tiles, r, share)
    mine = lax.dynamic_slice_in_dim(total, lax.axis_index("inner") * share, share, 2).astype(F32)
    basis = jnp.einsum("tde,tei->tdi", inverse, mine, precision=HIGHEST)
    image_out = jnp.einsum("tde,tei->tdi", inverse, summed, precision=HIGHEST)
    return (basis * math.sqrt(order), image_out)


def solution(mesh):
    return jax.shard_map(
        functools.partial(per_device, mesh.shape["tgt"], mesh.shape["inner"]),
        mesh=mesh,
        in_specs=(
            P(("tgt", "inner"), None, None),
            P(("tgt", "inner")),
            P(("tgt", "inner")),
            P(("tgt", "inner")),
            P(("tgt", "inner"), None, None),
            P(("tgt", "inner"), None, None),
            P(("tgt", "inner")),
            P(("tgt", "inner")),
            P(("tgt", "inner"), None, None),
            P(("tgt", "inner"), None, None),
            P("tgt"),
        ),
        out_specs=(P("tgt", None, "inner"), P("tgt", None, "inner")),
        check_vma=False,
    )
```

```python
import functools
import math

import jax
import jax.numpy as jnp
from jax import lax
from jax.experimental import pallas as pl
from jax.experimental.pallas import tpu as pltpu
from jax.sharding import PartitionSpec as P

HIGHEST = lax.Precision.HIGHEST
MESH = pl.DeviceIdType.MESH
F32 = jnp.float32
BF16 = jnp.bfloat16
VMEM_LIMIT = 56 * 1024 * 1024


def nt_dot(a, b):
    return lax.dot_general(a, b, (((1,), (1,)), ((), ())), preferred_element_type=F32)


def nn_dot(a, b):
    return lax.dot_general(a, b, (((1,), (0,)), ((), ())), preferred_element_type=F32)


def split(x):
    hi = x.astype(BF16)
    return hi, (x - hi.astype(F32)).astype(BF16)


def probe_tile(seed, shape):
    chan = lax.broadcasted_iota(jnp.int32, shape, 0)
    place = lax.broadcasted_iota(jnp.int32, shape, 1)
    code = lax.rem(
        seed * 9973
        + place * place * 7
        + place * chan * 131
        + chan * chan * 17
        + place * 7919
        + chan * 104729,
        jnp.full(shape, 65521, jnp.int32),
    )
    return ((code.astype(F32) - 32760.0) / 32768.0).astype(BF16)


def gather_kernel(nt, batch, low_right, near_right, count, seeds, u_ref, v_ref, low_v_ref, near_ref, *refs):
    sv_ref, mix_ref, lh_ref, ll_ref, probe_ref, su, sv, low_v, near, send, recv, local, out_sem = refs
    me = lax.axis_index("tgt")
    k = u_ref.shape[0]
    h = k // 2
    mine = pl.ds(me * k, k)
    loads = [
        pltpu.make_async_copy(u_ref, su.at[mine], local.at[0]),
        pltpu.make_async_copy(v_ref, sv.at[mine], local.at[1]),
        pltpu.make_async_copy(low_v_ref, low_v, local.at[2]),
        pltpu.make_async_copy(near_ref, near, local.at[3]),
    ]
    for c in loads:
        c.start()
    barrier = pltpu.get_barrier_semaphore()

    def push(src, dst, sem, to):
        copy = pltpu.make_async_remote_copy(
            src_ref=src,
            dst_ref=dst,
            send_sem=send.at[sem],
            recv_sem=recv.at[sem],
            device_id={"tgt": to},
            device_id_type=MESH,
        )
        copy.start()
        return copy

    def mix():
        loads[2].wait()

        def body(i, carry):
            for o in range(batch):
                j = i * batch + o
                mix_ref[j] = nt_dot(low_v[j], su[low_right[j]]).astype(BF16)
            return carry

        lax.fori_loop(0, low_v.shape[0] // batch, body, 0)

    def lefts():
        loads[3].wait()

        def body(j, carry):
            live = (j < count[0]).astype(F32)
            hi, lo = split(nt_dot(su[near_right[j]], near[j]) * live)
            lh_ref[j] = hi
            ll_ref[j] = lo
            return carry

        lax.fori_loop(0, near.shape[0], body, 0)

    def probes():
        def body(t, carry):
            probe_ref[t] = probe_tile(seeds[t], probe_ref.shape[1:])
            return carry

        lax.fori_loop(0, probe_ref.shape[0], body, 0)

    outs = []

    def emit(owner):
        rows = pl.ds(owner * k, k)
        c = pltpu.make_async_copy(sv.at[rows], sv_ref.at[rows], out_sem.at[len(outs)])
        c.start()
        outs.append(c)

    if nt == 4:
        a = me + 1 - 2 * (me % 2)
        b = (me + 2) % 4
        for peer in (a, b):
            pl.semaphore_signal(barrier, inc=1, device_id={"tgt": peer}, device_id_type=MESH)
        pl.semaphore_wait(barrier, 2)

        def own(src, dst, sem):
            low, high = pl.ds(0, h), pl.ds(h, k - h)
            at_low, at_high = pl.ds(me * k, h), pl.ds(me * k + h, k - h)
            return [
                push(src.at[low], dst.at[at_low], sem, a),
                push(src.at[high], dst.at[at_high], sem + 1, b),
                push(src.at[high], dst.at[at_high], sem + 2, a),
                push(src.at[low], dst.at[at_low], sem + 3, b),
            ]

        def onward(dst, copies, sem):
            from_a, from_b = pl.ds(a * k, h), pl.ds(b * k + h, k - h)
            copies[0].wait_recv()
            fa = push(dst.at[from_a], dst.at[from_a], sem, b)
            copies[1].wait_recv()
            return [fa, push(dst.at[from_b], dst.at[from_b], sem + 1, a)]

        us = own(u_ref, su, 0)
        probes()
        uf = onward(su, us, 4)
        vs = own(v_ref, sv, 6)
        for c in us[2:] + uf:
            c.wait_recv()
        loads[0].wait()
        mix()
        vf = onward(sv, vs, 10)
        lefts()
        for c in vs[2:]:
            c.wait_recv()
        loads[1].wait()
        for owner in (me, a, b):
            emit(owner)
        for c in vf:
            c.wait_recv()
        emit(a + b - me)
        copies = us + uf + vs + vf
    else:
        for d in range(1, nt):
            pl.semaphore_signal(
                barrier, inc=1, device_id={"tgt": (me + d) % nt}, device_id_type=MESH
            )
        pl.semaphore_wait(barrier, nt - 1)
        copies = []
        for d in range(1, nt):
            to = (me + d) % nt
            copies.append(push(u_ref, su.at[mine], 2 * d - 2, to))
            copies.append(push(v_ref, sv.at[mine], 2 * d - 1, to))
        probes()
        for c in copies:
            c.wait_recv()
        loads[0].wait()
        mix()
        lefts()
        loads[1].wait()
        for d in range(nt):
            emit((me + d) % nt)
    for c in copies:
        c.wait_send()
    for c in outs:
        c.wait()


def gather_tiles(nt, batch, low_right, near_right, count, seeds, u, v, low_v, near):
    sems = 12 if nt == 4 else max(2 * nt - 2, 1)
    seg = (nt * u.shape[0],) + u.shape[1:]
    r = u.shape[1]
    left = jax.ShapeDtypeStruct((near.shape[0], r, near.shape[1]), BF16)
    return pl.pallas_call(
        functools.partial(gather_kernel, nt, batch),
        out_shape=(
            jax.ShapeDtypeStruct(seg, v.dtype),
            jax.ShapeDtypeStruct((low_v.shape[0], low_v.shape[1], r), BF16),
            left,
            left,
            jax.ShapeDtypeStruct((seeds.shape[0], r, near.shape[1]), BF16),
        ),
        in_specs=[pl.BlockSpec(memory_space=pltpu.SMEM)] * 4
        + [pl.BlockSpec(memory_space=pl.ANY)] * 4,
        out_specs=[pl.BlockSpec(memory_space=pl.ANY)]
        + [pl.BlockSpec(memory_space=pltpu.VMEM)] * 4,
        scratch_shapes=[
            pltpu.VMEM(seg, u.dtype),
            pltpu.VMEM(seg, v.dtype),
            pltpu.VMEM(low_v.shape, low_v.dtype),
            pltpu.VMEM(near.shape, near.dtype),
            pltpu.SemaphoreType.DMA((sems,)),
            pltpu.SemaphoreType.DMA((sems,)),
            pltpu.SemaphoreType.DMA((4,)),
            pltpu.SemaphoreType.DMA((nt,)),
        ],
        compiler_params=pltpu.CompilerParams(
            collective_id=0, has_side_effects=True, vmem_limit_bytes=VMEM_LIMIT
        ),
    )(low_right, near_right, count, seeds, u, v, low_v, near)


def chol_inverse(s_ref, out_ref, a_ref):
    tiles, r, _ = s_ref.shape
    row = lax.broadcasted_iota(jnp.int32, (r, r), 0)
    col = lax.broadcasted_iota(jnp.int32, (r, r), 1)
    eye = (row == col).astype(F32)
    for t in range(tiles):
        s = s_ref[t]
        a_ref[t, :, :r] = nt_dot(s, s)
        a_ref[t, :, r:] = eye
    for base in range(0, r, 8):
        shape = (tiles, r - base, 2 * r)
        sub = lax.broadcasted_iota(jnp.int32, shape, 1) + base
        lane = lax.broadcasted_iota(jnp.int32, shape, 2)

        def body(k, carry):
            whole_a = a_ref[:, base:, :]
            pivot = a_ref[:, pl.ds(k, 1), :]
            column = jnp.sum(jnp.where(lane == k, whole_a, 0.0), axis=2, keepdims=True)
            diag = jnp.sum(jnp.where(lane[:, :1] == k, pivot, 0.0), axis=2, keepdims=True)
            step = column * (pivot / diag)
            a_ref[:, base:, :] = whole_a - jnp.where(sub > k, step, 0.0)
            return carry

        lax.fori_loop(base, base + 8, body, 0)
    a = a_ref[...]
    sub = lax.broadcasted_iota(jnp.int32, a.shape, 1)
    lane = lax.broadcasted_iota(jnp.int32, a.shape, 2)
    diag = jnp.sum(jnp.where(lane == sub, a, 0.0), axis=2, keepdims=True)
    out_ref[...] = (a * lax.rsqrt(diag))[:, :, r:]


def reduce_kernel(n, gather, x_ref, *refs):
    if gather:
        out_ref, half, cut, part, total, send, recv = refs
    else:
        s_ref, out_ref, inv_ref, half, cut, part, a_ref, send, recv = refs
    me = lax.axis_index("inner")
    m = n // 2
    z = me // 2
    core = me % 2
    other = 1 - core
    sib = z * 2 + other
    barrier = pltpu.get_barrier_semaphore()
    pl.semaphore_signal(barrier, inc=1, device_id={"inner": sib}, device_id_type=MESH)
    for d in range(1, m):
        peer = ((z + d) % m) * 2 + core
        pl.semaphore_signal(barrier, inc=1, device_id={"inner": peer}, device_id_type=MESH)
    pl.semaphore_wait(barrier, m)

    def push(src, dst, sem, to):
        copy = pltpu.make_async_remote_copy(
            src_ref=src,
            dst_ref=dst,
            send_sem=send.at[sem],
            recv_sem=recv.at[sem],
            device_id={"inner": to},
            device_id_type=MESH,
        )
        copy.start()
        return copy

    pairs = []
    for d in range(m):
        q = (z + 1 + d) % m
        pairs.append(push(x_ref.at[q, other], half.at[q], d, sib))
    sends = []
    for d in range(m):
        q = (z + 1 + d) % m
        pairs[d].wait_recv()
        if d < m - 1:
            cut[d] = (half[q] + x_ref[q, core]).astype(BF16)
            sends.append(push(cut.at[d], part.at[m - 2 - d], m + d, q * 2 + core))
    if not gather:
        chol_inverse(s_ref, inv_ref, a_ref)
    acc = half[z] + x_ref[z, core]
    for d in range(m - 1):
        sends[d].wait_recv()
        acc = acc + part[m - 2 - d].astype(F32)
    if gather:
        total[...] = acc.astype(BF16)
        out_ref[z, core] = acc.astype(BF16)
        outs = [push(total, out_ref.at[z, core], 2 * m - 1, sib)]
        away = []
        for d in range(m - 1):
            q = (z + 1 + d) % m
            away.append(push(total, out_ref.at[z, core], 2 * m + d, q * 2 + core))
        for d in range(m - 1):
            q = (z + 2 * m - 1 - d) % m
            away[d].wait_recv()
            outs.append(push(out_ref.at[q, core], out_ref.at[q, core], 3 * m - 1 + d, sib))
        for c in outs:
            c.wait_recv()
        sends = sends + outs + away
    else:
        out_ref[...] = acc
    for c in pairs + sends:
        c.wait_send()


def reduce_inner(n, x, gather, sketch=None):
    m = n // 2
    block = x.shape[2:]
    sems = 4 * m - 2 if gather else 2 * m - 1
    args = [x] if gather else [x, sketch]
    scratch = [pltpu.VMEM((m,) + block, F32)] + [pltpu.VMEM((max(m - 1, 1),) + block, BF16)] * 2
    vmem = pl.BlockSpec(memory_space=pltpu.VMEM)
    if gather:
        outs, specs = jax.ShapeDtypeStruct(x.shape, BF16), vmem
        scratch.append(pltpu.VMEM(block, BF16))
    else:
        tiles, r, _ = sketch.shape
        outs = (jax.ShapeDtypeStruct(block, F32), jax.ShapeDtypeStruct((tiles, r, r), F32))
        specs = (vmem, vmem)
        scratch.append(pltpu.VMEM((tiles, r, 2 * r), F32))
    return pl.pallas_call(
        functools.partial(reduce_kernel, n, gather),
        out_shape=outs,
        in_specs=[vmem] * len(args),
        out_specs=specs,
        scratch_shapes=scratch + [pltpu.SemaphoreType.DMA((sems,))] * 2,
        compiler_params=pltpu.CompilerParams(
            collective_id=1 if gather else 2, has_side_effects=True, vmem_limit_bytes=VMEM_LIMIT
        ),
    )(*args)


def both(x, axis):
    return jnp.concatenate([x, x], axis=axis)


def parts(x):
    return jnp.concatenate(split(x), axis=1)


def sketch_kernel(batch, slots, steps, right, target, near_right, near_target, *refs):
    v_refs = refs[:batch]
    low_u_ref, mix_ref, lh_ref, ll_ref, nv_ref, probe_ref, sk_ref = refs[batch:]
    j = pl.program_id(0)

    @pl.when(j == 0)
    def _():
        sk_ref[...] = jnp.zeros_like(sk_ref)

    def near_term():
        t = near_target[j]
        lh = lh_ref[0]
        zh, zl = split(nt_dot(probe_ref[t], nv_ref[0]))
        left = jnp.concatenate([lh, lh, ll_ref[0]], axis=0)
        sk_ref[t] += nn_dot(jnp.concatenate([zh, zl, zh], axis=1), left)

    span = range(batch)
    where = [target[j * batch + o] for o in span]
    zeta = [nt_dot(probe_ref[where[o]], v_refs[o][0]) for o in span]
    zeta = [parts(x) for x in zeta]
    q = [nt_dot(zeta[o], both(mix_ref[o], 1)) for o in span]
    q = [parts(x) for x in q]
    for o in span:
        sk_ref[where[o]] += nn_dot(q[o], both(low_u_ref[o], 0))
    if slots == steps:
        near_term()
    else:
        pl.when(j < slots)(near_term)


def add_columns(im_ref, t, y):
    n, share = im_ref.shape[0], im_ref.shape[3]
    for p in range(n):
        im_ref[p, t] += y[:, p * share : (p + 1) * share]


def image_kernel(batch, slots, steps, right, target, near_right, near_target, *refs):
    v_refs = refs[:batch]
    low_u_ref, mix_ref, lh_ref, ll_ref, nv_ref, sk_ref, im_ref = refs[batch:]
    j = pl.program_id(0)

    @pl.when(j == 0)
    def _():
        im_ref[...] = jnp.zeros_like(im_ref)

    def near_term():
        t = near_target[j]
        left = jnp.concatenate([lh_ref[0], ll_ref[0]], axis=1)
        proj = nt_dot(both(sk_ref[t], 1), left)
        add_columns(im_ref, t, nn_dot(parts(proj), both(nv_ref[0], 0)))

    span = range(batch)
    where = [target[j * batch + o] for o in span]
    w = [nt_dot(sk_ref[where[o]], low_u_ref[o]) for o in span]
    w = [parts(x) for x in w]
    proj = [nn_dot(w[o], both(mix_ref[o], 0)) for o in span]
    proj = [parts(x) for x in proj]
    for o in span:
        add_columns(im_ref, where[o], nn_dot(proj[o], both(v_refs[o][0], 0)))
    if slots == steps:
        near_term()
    else:
        pl.when(j < slots)(near_term)


def whole(shape):
    zeros = (0,) * len(shape)
    return pl.BlockSpec(shape, lambda j, *s: zeros)


def at_right(shape, batch, o):
    return pl.BlockSpec((1,) + shape[1:], lambda j, right, *s: (right[j * batch + o], 0, 0))


def at_near(shape, slots):
    return pl.BlockSpec(
        (1,) + shape[1:],
        lambda j, right, target, near, *s: (near[jnp.minimum(j, slots - 1)], 0, 0),
    )


def near_step(shape):
    return pl.BlockSpec(
        (1,) + shape[1:], lambda j, *s: (jnp.minimum(j, shape[0] - 1), 0, 0)
    )


def per_step(batch, shape):
    return pl.BlockSpec((batch,) + shape[1:], lambda j, *s: (j,) + (0,) * (len(shape) - 1))


def run(kernel, scalars, steps, ins, specs, outs, out_specs):
    return pl.pallas_call(
        kernel,
        grid_spec=pltpu.PrefetchScalarGridSpec(
            num_scalar_prefetch=len(scalars), grid=(steps,), in_specs=specs, out_specs=out_specs
        ),
        out_shape=outs,
        compiler_params=pltpu.CompilerParams(vmem_limit_bytes=VMEM_LIMIT),
    )(*scalars, *ins)


def per_device(
    nt,
    ni,
    near_tiles,
    near_target,
    near_right,
    near_count,
    low_u,
    low_v,
    low_target,
    low_right,
    right_u,
    right_v,
    probe_seed,
):
    slots, order = near_tiles.shape[0], near_tiles.shape[1]
    lows, r = low_u.shape[0], low_u.shape[1]
    tiles = probe_seed.shape[0]
    share = order // ni
    batch = math.gcd(lows, 8)
    while lows // batch < slots:
        batch = batch // 2
    steps = lows // batch
    seg_v, mixing, lh, ll, probe = gather_tiles(
        nt,
        batch,
        low_right,
        near_right,
        near_count,
        probe_seed,
        right_u,
        right_v,
        low_v,
        near_tiles,
    )
    sk = jax.ShapeDtypeStruct((tiles, r, order), F32)
    near_specs = [at_near(seg_v.shape, slots)]
    pair_specs = (
        [at_right(seg_v.shape, batch, o) for o in range(batch)]
        + [per_step(batch, low_u.shape), per_step(batch, mixing.shape)]
        + [near_step(lh.shape), near_step(ll.shape)]
        + near_specs
    )
    scalars = (low_right, low_target, near_right, near_target)
    pair_args = (seg_v,) * batch + (low_u, mixing, lh, ll, seg_v)
    sketch = run(
        functools.partial(sketch_kernel, batch, slots, steps),
        scalars,
        steps,
        pair_args + (probe,),
        pair_specs + [whole(probe.shape)],
        sk,
        whole(sk.shape),
    )
    rows = tiles * r // ni
    total = reduce_inner(ni, sketch.reshape(ni // 2, 2, rows, order), True)
    total = total.reshape(tiles, r, order)
    im = jax.ShapeDtypeStruct((ni, tiles, r, share), F32)
    image = run(
        functools.partial(image_kernel, batch, slots, steps),
        scalars,
        steps,
        pair_args + (total,),
        pair_specs + [whole(total.shape)],
        im,
        whole(im.shape),
    )
    summed, inverse = reduce_inner(
        ni, image.reshape(ni // 2, 2, tiles * r, share), False, total
    )
    summed = summed.reshape(tiles, r, share)
    mine = lax.dynamic_slice_in_dim(total, lax.axis_index("inner") * share, share, 2).astype(F32)
    basis = jnp.einsum("tde,tei->tdi", inverse, mine, precision=HIGHEST)
    image_out = jnp.einsum("tde,tei->tdi", inverse, summed, precision=HIGHEST)
    return (basis * math.sqrt(order), image_out)


def solution(mesh):
    return jax.shard_map(
        functools.partial(per_device, mesh.shape["tgt"], mesh.shape["inner"]),
        mesh=mesh,
        in_specs=(
            P(("tgt", "inner"), None, None),
            P(("tgt", "inner")),
            P(("tgt", "inner")),
            P(("tgt", "inner")),
            P(("tgt", "inner"), None, None),
            P(("tgt", "inner"), None, None),
            P(("tgt", "inner")),
            P(("tgt", "inner")),
            P(("tgt", "inner"), None, None),
            P(("tgt", "inner"), None, None),
            P("tgt"),
        ),
        out_specs=(P("tgt", None, "inner"), P("tgt", None, "inner")),
        check_vma=False,
    )
```
